32 devices in a mesh: src: 8 (over z, y), seg: 4 (over x, core).
Axes of the slice: x: 2, y: 2, z: 4, core: 2. Of those that a mesh axis runs over, the one named last changes fastest.
Arguments:
- residual: float32 [524288], P(('src', 'seg')), may hold values from -24 to 24
- obs_weight: float32 [524288], P(('src', 'seg')), may hold values from 0.25 to 4
- time_frac: float32 [524288], P(('src', 'seg')), may hold values from 0 to 0.99
- src_partials: float32 [5, 524288], P(None, ('src', 'seg')), may hold values from -6 to 6
- att_dir: float32 [3, 524288], P(None, ('src', 'seg')), may hold values from -6 to 6
- src_prior: float32 [5, 16384], P(None, 'src'), may hold values from 4 to 40
- att_prior: float32 [3, 2048], P(None, ('src', 'seg')), may hold values from 16 to 128
- obs_source: int32 [524288], P(('src', 'seg')), may hold values from 0 to 2047, as said below
- obs_interval: int32 [524288], P(('src', 'seg')), may hold values from 0 to 2047, as said below
- obs_count: int32 [32, 8], P(('src', 'seg')), may hold values from 256 to 2048, as said below
Outputs:
- src_update: float32 [5, 16384], P(None, 'src')
- att_update: float32 [3, 2048], P(None, ('src', 'seg'))
- residual_out: float32 [524288], P(('src', 'seg'))
The draws below stay inside these ranges and needn't reach their ends.
Inputs may be any that keep to these rules, and one draw needn't show every extreme that they name: obs_source of a slot on row r of obs_count (slot i with r = i // 16384) is the index of its source within the src block r // 4. A slot of row r in block b has an interval owned by knot block t = b * 4 + (r mod 4): obs_interval lies in t * 64 to (t + 1) * 64 - 1. `obs_count`: row r counts the live slots, from the start, of the 8 blocks of device r; for every seg index one block index is full (2048) on every row of that seg index.
All inputs are finite; a program needn't handle non-finite values.
Results may differ from the reference program's by a relative error of at most 0.0003.
Values sent between devices are 32-bit elements; how exact they have to be, the bound alone decides.
A program may use at most 128 MiB of HBM per device.

```python
import math
import jax
import jax.numpy as jnp
from jax import lax

SRC_DEV = 2048
OBS_DEV = 16384
KD = 64
ITERS_ATT = 6
CAP = 2048
S = 16384
NK = 2048
NOBS = 524288
N_SRC = 8
N_SEG = 4


def draw_obs_count(key, part):
    first_key, second_key = jax.random.split(jax.random.fold_in(key, 11))
    rows_total = N_SRC * N_SEG
    base_counts = jax.random.randint(first_key, (rows_total, N_SRC), CAP // 8, 3 * CAP // 4 + 1)
    busiest = jax.random.randint(second_key, (N_SEG,), 0, N_SRC)
    column_at = jnp.arange(rows_total, dtype=jnp.int32) % N_SEG
    destination_slot = jnp.take(busiest, column_at)
    full_block = jnp.arange(N_SRC, dtype=jnp.int32)[None, :] == destination_slot[:, None]
    return jnp.where(full_block, CAP, base_counts).astype(jnp.int32)


def draw_obs_source(key, part):
    picked = jax.random.randint(jax.random.fold_in(key, 23), (NOBS,), 0, SRC_DEV)
    return picked.astype(jnp.int32)


def draw_obs_interval(key, part):
    position = jnp.arange(NOBS, dtype=jnp.int32)
    seg_place = position // OBS_DEV % N_SEG
    dest_block = position % OBS_DEV // CAP
    owner = dest_block * N_SEG + seg_place
    picked = jax.random.randint(jax.random.fold_in(key, 37), (NOBS,), 0, KD)
    return (owner * KD + picked).astype(jnp.int32)


def levels(stream_key, dims, cuts, smallest, largest):
    def one(dim, shards_of):
        draws = jax.random.uniform(jax.random.fold_in(jax.random.fold_in(stream_key, 6), dim), (shards_of,), jnp.float32, smallest / len(cuts), largest / len(cuts))
        return jnp.repeat(jnp.exp(draws), dims[dim] // shards_of).reshape((-1,) + (1,) * (len(dims) - dim - 1))

    loudness = one(*cuts[0])
    for cut in cuts[1:]:
        loudness = loudness * one(*cut)
    return loudness


def normal_values(stream_key, extent, width, most, cuts=(), kind=jnp.bfloat16):
    drawn = width * jax.random.normal(stream_key, extent, jnp.float32)
    if cuts:
        drawn = drawn * levels(stream_key, extent, cuts, -0.22, 0.18)
    return jnp.clip(drawn, -most, most).astype(kind)


def setup_inputs(seed: int = 0) -> dict:
    keys = jax.random.split(jax.random.key(seed), 11)
    residual = normal_values(keys[0], (NOBS,), 4.0, 24.0, ((0, 32),), jnp.float32)
    obs_weight = jnp.clip(jnp.exp(math.log(4.0) - 2.7725887 * jax.random.uniform(keys[1], (NOBS,), jnp.float32) ** levels(keys[1], (NOBS,), ((0, 32),), -0.2, 0.2)), 0.25, 4.0)
    time_frac = jnp.clip(0.99 * jax.random.uniform(keys[2], (NOBS,), jnp.float32) ** levels(keys[2], (NOBS,), ((0, 32),), -0.2, 0.2), 0.0, 0.99)
    src_partials = normal_values(keys[3], (5, NOBS), 1.0, 6.0, ((1, 32),), jnp.float32)
    att_dir = normal_values(keys[4], (3, NOBS), 1.0, 6.0, ((1, 32),), jnp.float32)
    src_prior = jnp.clip(jnp.exp(math.log(40.0) - 2.3025851 * jax.random.uniform(keys[5], (5, S), jnp.float32) ** levels(keys[5], (5, S), ((1, 8),), -0.2, 0.2)), 4.0, 40.0)
    att_prior = jnp.clip(jnp.exp(math.log(128.0) - 2.0794415 * jax.random.uniform(keys[6], (3, NK), jnp.float32) ** levels(keys[6], (3, NK), ((1, 32),), -0.2, 0.2)), 16.0, 128.0)
    obs_source = draw_obs_source(jax.random.fold_in(keys[10], 71), 0)
    obs_interval = draw_obs_interval(jax.random.fold_in(keys[10], 71), 0)
    obs_count = draw_obs_count(jax.random.fold_in(keys[10], 71), 0)
    return {"residual": residual, "obs_weight": obs_weight, "time_frac": time_frac, "src_partials": src_partials, "att_dir": att_dir, "src_prior": src_prior, "att_prior": att_prior, "obs_source": obs_source, "obs_interval": obs_interval, "obs_count": obs_count}


param_pairs = [(0, 0), (0, 1), (0, 2), (0, 3), (0, 4), (1, 1), (1, 2), (1, 3), (1, 4), (2, 2), (2, 3), (2, 4), (3, 3), (3, 4), (4, 4)]
sym_pairs = [(0, 0), (0, 1), (0, 2), (1, 1), (1, 2), (2, 2)]
damping = 0.5

def cholesky_solve5(normal, rhs_terms, prior_diag):
    matrix = {}
    for number, pair_at in enumerate(param_pairs):
        matrix[pair_at] = normal[number]
        matrix[pair_at[1], pair_at[0]] = normal[number]
    for number in range(5):
        matrix[number, number] = matrix[number, number] + prior_diag[number]
    factor = {}
    for row_at in range(5):
        for col_at in range(row_at + 1):
            running = matrix[row_at, col_at]
            for inner_k in range(col_at):
                running = running - factor[row_at, inner_k] * factor[col_at, inner_k]
            if row_at == col_at:
                factor[row_at, row_at] = jnp.sqrt(running)
            else:
                factor[row_at, col_at] = running / factor[col_at, col_at]
    forward = []
    for row_at in range(5):
        running = rhs_terms[row_at]
        for inner_k in range(row_at):
            running = running - factor[row_at, inner_k] * forward[inner_k]
        forward.append(running / factor[row_at, row_at])
    backward = [None] * 5
    for row_at in reversed(range(5)):
        running = forward[row_at]
        for inner_k in range(row_at + 1, 5):
            running = running - factor[inner_k, row_at] * backward[inner_k]
        backward[row_at] = running / factor[row_at, row_at]
    return jnp.stack(backward)

def spline_basis(local_time):
    floor_part = jnp.floor(local_time)
    frac_part = local_time - floor_part
    square = frac_part * frac_part
    cube_term = square * frac_part
    rest = 1.0 - frac_part
    splines = [rest * rest * rest / 6.0, (3.0 * cube_term - 6.0 * square + 4.0) / 6.0, (-3.0 * cube_term + 3.0 * square + 3.0 * frac_part + 1.0) / 6.0, cube_term / 6.0]
    return (floor_part.astype(jnp.int32), splines)

def knot_term(weight, first_pass, splines, direction, spline_at, stack_axis):
    outer_terms = []
    for left_at, right_at in sym_pairs:
        outer_terms.append(weight * direction[left_at] * direction[right_at])
    rows_out = []
    for offset in range(4):
        if spline_at + offset <= 3:
            coeff_pair = splines[spline_at] * splines[spline_at + offset]
            for entry_term in outer_terms:
                rows_out.append(coeff_pair * entry_term)
        else:
            for entry_term in outer_terms:
                rows_out.append(jnp.zeros_like(entry_term))
    scaled = weight * splines[spline_at] * first_pass
    for axis_at in range(3):
        rows_out.append(scaled * direction[axis_at])
    return jnp.stack(rows_out, stack_axis)

def sym_apply(entries, vector):
    first_row = entries[0] * vector[0] + entries[1] * vector[1] + entries[2] * vector[2]
    middle_row_entries = entries[1] * vector[0] + entries[3] * vector[1] + entries[4] * vector[2]
    third_row = entries[2] * vector[0] + entries[4] * vector[1] + entries[5] * vector[2]
    return jnp.stack([first_row, middle_row_entries, third_row])

def symmetric_inverse(entries):
    cof_00 = entries[3] * entries[5] - entries[4] * entries[4]
    cof_01 = entries[2] * entries[4] - entries[1] * entries[5]
    cof_02 = entries[1] * entries[4] - entries[2] * entries[3]
    cof_11 = entries[0] * entries[5] - entries[2] * entries[2]
    cof_12 = entries[1] * entries[2] - entries[0] * entries[4]
    cof_22 = entries[0] * entries[3] - entries[1] * entries[1]
    determinant = entries[0] * cof_00 + entries[1] * cof_01 + entries[2] * cof_02
    return jnp.stack([cof_00, cof_01, cof_02, cof_11, cof_12, cof_22]) / determinant

def add_prior(diag_sums, prior_diag):
    return jnp.stack([diag_sums[0] + prior_diag[0], diag_sums[1], diag_sums[2], diag_sums[3] + prior_diag[1], diag_sums[4], diag_sums[5] + prior_diag[2]])

def apply_operator(diag_block, upper_triangle_filled, vector_padded, knot_count):
    applied = sym_apply(diag_block, vector_padded[:, 3:3 + knot_count])
    for offset in range(1, 4):
        upper_here = upper_triangle_filled[6 * (offset - 1):6 * offset, 3:3 + knot_count]
        upper_left = upper_triangle_filled[6 * (offset - 1):6 * offset, 3 - offset:3 - offset + knot_count]
        applied = applied + sym_apply(upper_here, vector_padded[:, 3 + offset:3 + offset + knot_count])
        applied = applied + sym_apply(upper_left, vector_padded[:, 3 - offset:3 - offset + knot_count])
    return applied

def table_correction(full_table, interval, splines, direction):
    padded = jnp.pad(full_table, ((0, 0), (1, 2)))
    correction = jnp.zeros(interval.shape, jnp.float32)
    for spline_at in range(4):
        looked = jnp.take(padded, interval + spline_at, axis=1)
        correction = correction + splines[spline_at] * lax.optimization_barrier(jnp.sum(direction * looked, 0))
    return correction

def reference(residual, obs_weight, time_frac, src_partials, att_dir, src_prior, att_prior, obs_source, obs_interval, obs_count):
    total_obs = residual.shape[0]
    position = jnp.arange(total_obs, dtype=jnp.int32)
    device_at = position // OBS_DEV
    block_at = position % OBS_DEV // CAP
    slot_at = position % CAP
    live_mask = (slot_at < obs_count[device_at, block_at]).astype(jnp.float32)
    weight = obs_weight * live_mask
    global_source = (device_at // N_SEG * SRC_DEV + obs_source).astype(jnp.int32)
    features = []
    for left_at, right_at in param_pairs:
        features.append(weight * src_partials[left_at] * src_partials[right_at])
    for axis_at in range(5):
        features.append(weight * src_partials[axis_at] * residual)
    src_sums = jax.ops.segment_sum(jnp.stack(features, 1), global_source, num_segments=S).T
    src_update = cholesky_solve5(src_sums[:15], src_sums[15:], src_prior)
    src_corr = lax.optimization_barrier(jnp.sum(src_partials * jnp.take(src_update, global_source, axis=1), 0))
    first_pass = residual - src_corr
    local_time = (obs_interval % KD).astype(jnp.float32) + time_frac
    floor_at, splines = spline_basis(local_time)
    knot_sums = jnp.zeros((NK + 3, 27), jnp.float32)
    for spline_at in range(4):
        term = knot_term(weight, first_pass, splines, att_dir, spline_at, 1)
        knot_sums = knot_sums + jax.ops.segment_sum(term, obs_interval + spline_at, num_segments=NK + 3)
    own_sums = knot_sums[1:NK + 1].T
    diag_block = add_prior(own_sums[:6], att_prior)
    inverse = symmetric_inverse(diag_block)
    upper_triangle_filled = jnp.pad(own_sums[6:24], ((0, 0), (3, 0)))
    att_rhs = own_sums[24:27]
    att_update = jnp.zeros((3, NK), jnp.float32)
    for sweep_at in range(ITERS_ATT):
        vector_padded = jnp.pad(att_update, ((0, 0), (3, 3)))
        att_update = att_update + damping * sym_apply(inverse, att_rhs - apply_operator(diag_block, upper_triangle_filled, vector_padded, NK))
    att_corr = table_correction(att_update, obs_interval, splines, att_dir)
    residual_out = residual - live_mask * (src_corr + att_corr)
    return (src_update, att_update, residual_out)
```

```python
import functools

import jax
import jax.numpy as jnp
from jax import lax
from jax.experimental import pallas as pl
from jax.experimental.pallas import tpu as pltpu
from jax.sharding import PartitionSpec as P

ITERS_ATT = 6
LO = 256
LANES = 128
F32 = jnp.float32
BF16 = jnp.bfloat16
PAIR_ROW = {}
for _d in range(3):
    for _p in range(5):
        _q = (_p + _d) % 5
        PAIR_ROW[_p, _q] = 5 * _d + _p
        PAIR_ROW[_q, _p] = 5 * _d + _p
damping = 0.5
vmem = pl.BlockSpec(memory_space=pltpu.VMEM)
smem = pl.BlockSpec(memory_space=pltpu.SMEM)


def split_rows(values):
    high = values.astype(BF16).astype(F32)
    return jnp.concatenate([high, values - high], 0).astype(BF16)


def contract_lanes(left, right):
    return lax.dot_general(left, right, (((1,), (1,)), ((), ())), preferred_element_type=F32)


def matmul(left, right):
    return lax.dot_general(left, right, (((1,), (0,)), ((), ())), preferred_element_type=F32)


def one_hot(index_row, rows):
    ids = lax.broadcasted_iota(jnp.int32, (rows, index_row.shape[1]), 0)
    return jnp.where(ids == index_row, 1.0, 0.0).astype(BF16)


def live_weight(weight_row, count):
    place = lax.broadcasted_iota(jnp.int32, weight_row.shape, 1)
    return jnp.where(place < count, weight_row, 0.0)


def basis(interval_row, frac_row, knots):
    local_time = (interval_row % knots).astype(F32) + frac_row
    floor_part = jnp.floor(local_time)
    u = local_time - floor_part
    square = u * u
    cube = square * u
    rest = 1.0 - u
    splines = [
        rest * rest * rest / 6.0,
        (3.0 * cube - 6.0 * square + 4.0) / 6.0,
        (-3.0 * cube + 3.0 * square + 3.0 * u + 1.0) / 6.0,
        cube / 6.0,
    ]
    return floor_part.astype(jnp.int32), splines


def source_sums_block(partials, weight, residual, source, hot):
    width = partials.shape[1]
    weighted = partials * weight
    features = jnp.concatenate(
        [
            weighted * partials,
            weighted * jnp.concatenate([partials[1:], partials[:1]], 0),
            weighted * jnp.concatenate([partials[2:], partials[:2]], 0),
            weighted * residual,
            jnp.zeros((4, width), F32),
        ],
        0,
    )
    return split_rows(features)


def expand(split, high_row, groups):
    width = split.shape[1]
    high16 = jnp.broadcast_to(high_row, (16, width))
    parts = []
    for group in range(groups):
        mask = jnp.where(high16 == group, 1.0, 0.0).astype(BF16)
        for start in range(0, split.shape[0], 16):
            parts.append(split[start : start + 16] * mask)
    return jnp.concatenate(parts, 0)


def normal_block(direction, weight, splines, hot):
    blank = jnp.zeros((2, direction.shape[1]), F32)
    d0, d1, d2 = direction[0:1], direction[1:2], direction[2:3]
    entries = (
        weight
        * jnp.concatenate([d0, d0, d0, d1, d1, d2, blank], 0)
        * jnp.concatenate([d0, d1, d2, d1, d2, d2, blank], 0)
    )
    groups = []
    for at in range(4):
        for offset in range(4 - at):
            groups.append((splines[at] * splines[at + offset]) * entries)
    rows = 8 * len(groups)
    sums = contract_lanes(split_rows(jnp.concatenate(groups, 0)), hot)
    sums = sums[:rows] + sums[rows:]
    upper = [None] * 4
    number = 0
    for at in range(4):
        for offset in range(4 - at):
            term = sums[8 * number : 8 * number + 8]
            term = term if at == 0 else pltpu.roll(term, at, 1)
            upper[offset] = term if upper[offset] is None else upper[offset] + term
            number += 1
    return jnp.concatenate([term[:6] for term in upper], 0)


def rhs_block(direction, weighted_first, splines, hot):
    base = jnp.concatenate(
        [direction * weighted_first, jnp.zeros((5, direction.shape[1]), F32)], 0
    )
    sums = contract_lanes(split_rows(jnp.concatenate([s * base for s in splines], 0)), hot)
    sums = sums[:32] + sums[32:]
    total = sums[:8]
    for at in range(1, 4):
        total = total + pltpu.roll(sums[8 * at : 8 * at + 8], at, 1)
    return total


def cholesky_solve5(sums, prior):
    factor = {}
    for row in range(5):
        for col in range(row + 1):
            at = PAIR_ROW[row, col]
            running = sums[at : at + 1]
            if row == col:
                running = running + prior[row : row + 1]
            for k in range(col):
                running = running - factor[row, k] * factor[col, k]
            if row == col:
                factor[row, row] = jnp.sqrt(running)
            else:
                factor[row, col] = running / factor[col, col]
    forward = []
    for row in range(5):
        running = sums[15 + row : 16 + row]
        for k in range(row):
            running = running - factor[row, k] * forward[k]
        forward.append(running / factor[row, row])
    backward = [None] * 5
    for row in reversed(range(5)):
        running = forward[row]
        for k in range(row + 1, 5):
            running = running - factor[k, row] * backward[k]
        backward[row] = running / factor[row, row]
    return jnp.concatenate(backward + [jnp.zeros((3, LO), F32)], 0)


def source_lookup(table, hot, high_row, partials):
    groups = table.shape[0] // 16
    looked = matmul(table, hot)
    half = 8 * groups
    high8 = jnp.broadcast_to(high_row, (8, hot.shape[1]))
    chosen = None
    for group in range(groups):
        term = looked[8 * group : 8 * group + 8] + looked[half + 8 * group : half + 8 * group + 8]
        term = jnp.where(high8 == group, term, 0.0)
        chosen = term if chosen is None else chosen + term
    return jnp.sum(partials * chosen[:5], 0, keepdims=True)


def attitude_lookup(window, shift, hot, splines, direction):
    tables = [pltpu.roll(window, LANES - (shift + at), 1) for at in range(4)]
    looked = matmul(split_rows(jnp.concatenate(tables, 0)), hot)
    looked = looked[:32] + looked[32:]
    total = None
    for at in range(4):
        term = splines[at] * looked[8 * at : 8 * at + 3]
        total = term if total is None else total + term
    return jnp.sum(direction * total, 0, keepdims=True)


def sym_apply(e, v):
    return [
        e[0] * v[0] + e[1] * v[1] + e[2] * v[2],
        e[1] * v[0] + e[3] * v[1] + e[4] * v[2],
        e[2] * v[0] + e[4] * v[1] + e[5] * v[2],
    ]


def symmetric_inverse(e):
    c00 = e[3] * e[5] - e[4] * e[4]
    c01 = e[2] * e[4] - e[1] * e[5]
    c02 = e[1] * e[4] - e[2] * e[3]
    c11 = e[0] * e[5] - e[2] * e[2]
    c12 = e[1] * e[2] - e[0] * e[4]
    c22 = e[0] * e[3] - e[1] * e[1]
    det = e[0] * c00 + e[1] * c01 + e[2] * c02
    return [c / det for c in (c00, c01, c02, c11, c12, c22)]


def window_of(before, own, after, halo, knots):
    lane = lax.broadcasted_iota(jnp.int32, own.shape, 1)
    left = pltpu.roll(before, (halo - 1 - knots) % LANES, 1)
    right = pltpu.roll(after, (halo - 1 + knots) % LANES, 1)
    total = pltpu.roll(own, halo - 1, 1)
    total = total + jnp.where(lane < halo + 2, left, 0.0)
    return total + jnp.where(lane >= halo - 1 + knots, right, 0.0)


def knot_valid(me, halo, knots, total):
    lane = lax.broadcasted_iota(jnp.int32, (1, LANES), 1)
    knot = me * knots + lane - halo
    return (knot >= 0) & (knot < total)


def prepare(normals, valid):
    rows = [jnp.where(valid, normals[i : i + 1], 0.0) for i in range(24)]
    diag = [jnp.where(valid, rows[i], 1.0 if i in (0, 3, 5) else 0.0) for i in range(6)]
    inverse = [jnp.where(valid, x, 0.0) for x in symmetric_inverse(diag)]
    return diag, rows, inverse


def sweeps(diag, rows, inverse, rhs):
    update = [damping * x for x in sym_apply(inverse, rhs)]
    for _ in range(1, ITERS_ATT):
        applied = sym_apply(diag, update)
        for offset in range(1, 4):
            upper = rows[6 * offset : 6 * offset + 6]
            ahead = [pltpu.roll(x, LANES - offset, 1) for x in update]
            behind = [pltpu.roll(x, offset, 1) for x in sym_apply(upper, update)]
            for at, x in enumerate(sym_apply(upper, ahead)):
                applied[at] = applied[at] + x + behind[at]
        step = sym_apply(inverse, [rhs[at] - applied[at] for at in range(3)])
        update = [update[at] + damping * step[at] for at in range(3)]
    return update


def block_slice(block, width):
    return pl.ds(pl.multiple_of(block * width, 128), width)


def sums_kernel(knots, res, ow, tf, sp, ad, osrc, oint, cnt, out_sums, out_norm, acc):
    blocks = cnt.shape[1]
    width = res.shape[1] // blocks
    groups = out_sums.shape[0]
    acc[...] = jnp.zeros_like(acc)

    def step(block, carry):
        sl = block_slice(block, width)
        weight = live_weight(ow[:, sl], cnt[0, block])
        source = osrc[:, sl]
        hot = one_hot(source % LO, LO)
        split = source_sums_block(sp[:, sl], weight, res[:, sl], source, hot)
        acc[...] += contract_lanes(expand(split, source // LO, groups), hot)
        floor_at, splines = basis(oint[:, sl], tf[:, sl], knots)
        out_norm[block] = normal_block(ad[:, sl], weight, splines, one_hot(floor_at, LANES))
        return carry

    lax.fori_loop(0, blocks, step, 0)
    for group in range(groups):
        out_sums[group] = acc[48 * group : 48 * group + 24] + acc[48 * group + 24 : 48 * group + 48]


def solve_kernel(sums, prior, out):
    for group in range(sums.shape[0]):
        out[group] = cholesky_solve5(sums[group], prior[:, group * LO : (group + 1) * LO])


def first_kernel(knots, upd, res, ow, tf, sp, ad, osrc, oint, cnt, out_upd, out_corr, out_rhs):
    blocks = cnt.shape[1]
    width = res.shape[1] // blocks
    groups = upd.shape[0]
    for group in range(groups):
        out_upd[:, group * LO : (group + 1) * LO] = upd[group, :5]
    table = split_rows(jnp.concatenate([upd[group] for group in range(groups)], 0))

    def step(block, carry):
        sl = block_slice(block, width)
        weight = live_weight(ow[:, sl], cnt[0, block])
        source = osrc[:, sl]
        corr = source_lookup(table, one_hot(source % LO, LO), source // LO, sp[:, sl])
        out_corr[:, sl] = corr
        floor_at, splines = basis(oint[:, sl], tf[:, sl], knots)
        out_rhs[block] = rhs_block(
            ad[:, sl], weight * (res[:, sl] - corr), splines, one_hot(floor_at, LANES)
        )
        return carry

    lax.fori_loop(0, blocks, step, 0)


def sweep_kernel(knots, total, halo, before, own, after, out_window, out_own):
    me = lax.axis_index("src") * lax.axis_size("seg") + lax.axis_index("seg")
    window = window_of(before[...], own[...], after[...], halo, knots)
    valid = knot_valid(me, halo, knots, total)
    diag, rows, inverse = prepare(window, valid)
    rhs = [jnp.where(valid, window[24 + at : 25 + at], 0.0) for at in range(3)]
    update = sweeps(diag, rows, inverse, rhs)
    final = jnp.concatenate(update + [jnp.zeros((5, LANES), F32)], 0)
    out_window[...] = final
    out_own[...] = pltpu.roll(final, LANES - halo, 1)[:3, :knots]


def last_kernel(knots, halo, windows, corr, res, tf, ad, oint, cnt, out):
    blocks = cnt.shape[1]
    width = res.shape[1] // blocks

    def step(block, carry):
        sl = block_slice(block, width)
        floor_at, splines = basis(oint[:, sl], tf[:, sl], knots)
        att = attitude_lookup(
            windows[block], halo - 1, one_hot(floor_at, LANES), splines, ad[:, sl]
        )
        residual = res[:, sl]
        out[:, sl] = residual - live_weight(corr[:, sl] + att, cnt[0, block])
        return carry

    lax.fori_loop(0, blocks, step, 0)


def call(kernel, outs, n_vmem, count=False, scratch=()):
    return pl.pallas_call(
        kernel,
        out_shape=[jax.ShapeDtypeStruct(shape, F32) for shape in outs],
        in_specs=[vmem] * n_vmem + [smem] * count,
        out_specs=[vmem] * len(outs),
        scratch_shapes=list(scratch),
        compiler_params=pltpu.CompilerParams(vmem_limit_bytes=40 * 2**20),
    )


def body(residual, obs_weight, time_frac, src_partials, att_dir, src_prior, att_prior,
         obs_source, obs_interval, obs_count):
    n_src = lax.axis_size("src")
    n_seg = lax.axis_size("seg")
    seg_at = lax.axis_index("seg")
    obs = residual.shape[0]
    sources = src_prior.shape[1]
    knots = att_prior.shape[1]
    total = knots * n_src * n_seg
    groups = sources // LO
    halo = 32
    rows = [x.reshape(1, obs) for x in (residual, obs_weight, time_frac, obs_source, obs_interval)]
    res, ow, tf, osrc, oint = rows
    sums, normals = call(
        functools.partial(sums_kernel, knots),
        [(groups, 24, LO), (n_src, 24, LANES)], 7, True, [pltpu.VMEM((groups * 48, LO), F32)],
    )(res, ow, tf, src_partials, att_dir, osrc, oint, obs_count)
    part = lax.psum_scatter(sums, "seg", scatter_dimension=0, tiled=True)
    share = sources // n_seg
    prior = lax.dynamic_slice_in_dim(src_prior, seg_at * share, share, 1)
    (upd,) = call(solve_kernel, [(groups // n_seg, 8, LO)], 2)(part, prior)
    upd = lax.all_gather(upd, "seg", axis=0, tiled=True)
    src_update, corr, rhs = call(
        functools.partial(first_kernel, knots),
        [(5, sources), (1, obs), (n_src, 8, LANES)], 8, True,
    )(upd, res, ow, tf, src_partials, att_dir, osrc, oint, obs_count)
    sent = jnp.concatenate([normals, rhs], 1)
    own = jnp.sum(lax.all_to_all(sent, "src", split_axis=0, concat_axis=0, tiled=True), 0)
    prior_ext = jnp.pad(att_prior, ((0, 0), (1, LANES - 1 - knots)))
    own = own.at[0].add(prior_ext[0]).at[3].add(prior_ext[1]).at[5].add(prior_ext[2])
    count = n_src * n_seg
    before = lax.ppermute(own, ("src", "seg"), [(i, i + 1) for i in range(count - 1)])
    after = lax.ppermute(own, ("src", "seg"), [(i + 1, i) for i in range(count - 1)])
    window, att_update = call(
        functools.partial(sweep_kernel, knots, total, halo), [(8, LANES), (3, knots)], 3
    )(before, own, after)
    windows = lax.all_gather(window, "src", axis=0)
    (out,) = call(functools.partial(last_kernel, knots, halo), [(1, obs)], 6, True)(
        windows, corr, res, tf, att_dir, oint, obs_count
    )
    return src_update, att_update, out.reshape(obs)


def solution(mesh):
    both = P(("src", "seg"))
    wide = P(None, ("src", "seg"))
    in_specs = (both, both, both, wide, wide, P(None, "src"), wide, both, both,
                P(("src", "seg"), None))
    out_specs = (P(None, "src"), wide, both)
    return jax.shard_map(body, mesh=mesh, in_specs=in_specs, out_specs=out_specs, check_vma=False)
```

```python
import functools

import jax
import jax.numpy as jnp
from jax import lax
from jax.experimental import pallas as pl
from jax.experimental.pallas import tpu as pltpu
from jax.sharding import PartitionSpec as P

ITERS_ATT = 6
LO = 256
LANES = 128
F32 = jnp.float32
BF16 = jnp.bfloat16
PAIR_ROW = {}
for _d in range(3):
    for _p in range(5):
        _q = (_p + _d) % 5
        PAIR_ROW[_p, _q] = 5 * _d + _p
        PAIR_ROW[_q, _p] = 5 * _d + _p
damping = 0.5
vmem = pl.BlockSpec(memory_space=pltpu.VMEM)
smem = pl.BlockSpec(memory_space=pltpu.SMEM)


def split_rows(values):
    high = values.astype(BF16).astype(F32)
    return jnp.concatenate([high, values - high], 0).astype(BF16)


def contract_lanes(left, right):
    return lax.dot_general(left, right, (((1,), (1,)), ((), ())), preferred_element_type=F32)


def matmul(left, right):
    return lax.dot_general(left, right, (((1,), (0,)), ((), ())), preferred_element_type=F32)


def one_hot(index_row, rows):
    ids = lax.broadcasted_iota(jnp.int32, (rows, index_row.shape[1]), 0)
    return jnp.where(ids == index_row, 1.0, 0.0).astype(BF16)


def live_weight(weight_row, count):
    place = lax.broadcasted_iota(jnp.int32, weight_row.shape, 1)
    return jnp.where(place < count, weight_row, 0.0)


def basis(interval_row, frac_row, knots):
    local_time = (interval_row % knots).astype(F32) + frac_row
    floor_part = jnp.floor(local_time)
    u = local_time - floor_part
    square = u * u
    cube = square * u
    rest = 1.0 - u
    splines = [
        rest * rest * rest / 6.0,
        (3.0 * cube - 6.0 * square + 4.0) / 6.0,
        (-3.0 * cube + 3.0 * square + 3.0 * u + 1.0) / 6.0,
        cube / 6.0,
    ]
    return floor_part.astype(jnp.int32), splines


def source_sums_block(partials, weight, residual, source, hot):
    width = partials.shape[1]
    weighted = partials * weight
    features = jnp.concatenate(
        [
            weighted * partials,
            weighted * jnp.concatenate([partials[1:], partials[:1]], 0),
            weighted * jnp.concatenate([partials[2:], partials[:2]], 0),
            weighted * residual,
            jnp.zeros((4, width), F32),
        ],
        0,
    )
    return split_rows(features)


def expand(split, high_row, groups):
    width = split.shape[1]
    high16 = jnp.broadcast_to(high_row, (16, width))
    parts = []
    for group in range(groups):
        mask = jnp.where(high16 == group, 1.0, 0.0).astype(BF16)
        for start in range(0, split.shape[0], 16):
            parts.append(split[start : start + 16] * mask)
    return jnp.concatenate(parts, 0)


def normal_block(direction, weight, splines, hot):
    blank = jnp.zeros((2, direction.shape[1]), F32)
    d0, d1, d2 = direction[0:1], direction[1:2], direction[2:3]
    entries = (
        weight
        * jnp.concatenate([d0, d0, d0, d1, d1, d2, blank], 0)
        * jnp.concatenate([d0, d1, d2, d1, d2, d2, blank], 0)
    )
    groups = []
    for at in range(4):
        for offset in range(4 - at):
            groups.append((splines[at] * splines[at + offset]) * entries)
    rows = 8 * len(groups)
    sums = contract_lanes(split_rows(jnp.concatenate(groups, 0)), hot)
    sums = sums[:rows] + sums[rows:]
    upper = [None] * 4
    number = 0
    for at in range(4):
        for offset in range(4 - at):
            term = sums[8 * number : 8 * number + 8]
            term = term if at == 0 else pltpu.roll(term, at, 1)
            upper[offset] = term if upper[offset] is None else upper[offset] + term
            number += 1
    return jnp.concatenate([term[:6] for term in upper], 0)


def rhs_block(direction, weighted_first, splines, hot):
    base = jnp.concatenate(
        [direction * weighted_first, jnp.zeros((5, direction.shape[1]), F32)], 0
    )
    sums = contract_lanes(split_rows(jnp.concatenate([s * base for s in splines], 0)), hot)
    sums = sums[:32] + sums[32:]
    total = sums[:8]
    for at in range(1, 4):
        total = total + pltpu.roll(sums[8 * at : 8 * at + 8], at, 1)
    return total


def cholesky_solve5(sums, prior):
    factor = {}
    for row in range(5):
        for col in range(row + 1):
            at = PAIR_ROW[row, col]
            running = sums[at : at + 1]
            if row == col:
                running = running + prior[row : row + 1]
            for k in range(col):
                running = running - factor[row, k] * factor[col, k]
            if row == col:
                factor[row, row] = jnp.sqrt(running)
            else:
                factor[row, col] = running / factor[col, col]
    forward = []
    for row in range(5):
        running = sums[15 + row : 16 + row]
        for k in range(row):
            running = running - factor[row, k] * forward[k]
        forward.append(running / factor[row, row])
    backward = [None] * 5
    for row in reversed(range(5)):
        running = forward[row]
        for k in range(row + 1, 5):
            running = running - factor[k, row] * backward[k]
        backward[row] = running / factor[row, row]
    return jnp.concatenate(backward + [jnp.zeros((3, LO), F32)], 0)


def source_lookup(table, hot, high_row, partials):
    groups = table.shape[0] // 16
    looked = matmul(table, hot)
    half = 8 * groups
    high8 = jnp.broadcast_to(high_row, (8, hot.shape[1]))
    chosen = None
    for group in range(groups):
        term = looked[8 * group : 8 * group + 8] + looked[half + 8 * group : half + 8 * group + 8]
        term = jnp.where(high8 == group, term, 0.0)
        chosen = term if chosen is None else chosen + term
    return jnp.sum(partials * chosen[:5], 0, keepdims=True)


def attitude_lookup(window, shift, hot, splines, direction):
    tables = [pltpu.roll(window, LANES - (shift + at), 1) for at in range(4)]
    looked = matmul(split_rows(jnp.concatenate(tables, 0)), hot)
    looked = looked[:32] + looked[32:]
    total = None
    for at in range(4):
        term = splines[at] * looked[8 * at : 8 * at + 3]
        total = term if total is None else total + term
    return jnp.sum(direction * total, 0, keepdims=True)


def sym_apply(e, v):
    return [
        e[0] * v[0] + e[1] * v[1] + e[2] * v[2],
        e[1] * v[0] + e[3] * v[1] + e[4] * v[2],
        e[2] * v[0] + e[4] * v[1] + e[5] * v[2],
    ]


def symmetric_inverse(e):
    c00 = e[3] * e[5] - e[4] * e[4]
    c01 = e[2] * e[4] - e[1] * e[5]
    c02 = e[1] * e[4] - e[2] * e[3]
    c11 = e[0] * e[5] - e[2] * e[2]
    c12 = e[1] * e[2] - e[0] * e[4]
    c22 = e[0] * e[3] - e[1] * e[1]
    det = e[0] * c00 + e[1] * c01 + e[2] * c02
    return [c / det for c in (c00, c01, c02, c11, c12, c22)]


def window_of(before, own, after, halo, knots, me, count):
    lane = lax.broadcasted_iota(jnp.int32, own.shape, 1)
    left = pltpu.roll(before, (halo - 1 - knots) % LANES, 1)
    right = pltpu.roll(after, (halo - 1 + knots) % LANES, 1)
    total = pltpu.roll(own, halo - 1, 1)
    total = total + jnp.where((lane < halo + 2) & (me > 0), left, 0.0)
    return total + jnp.where((lane >= halo - 1 + knots) & (me < count - 1), right, 0.0)


def knot_valid(me, halo, knots, total):
    lane = lax.broadcasted_iota(jnp.int32, (1, LANES), 1)
    knot = me * knots + lane - halo
    return (knot >= 0) & (knot < total)


def prepare(normals, valid):
    rows = [jnp.where(valid, normals[i : i + 1], 0.0) for i in range(24)]
    diag = [jnp.where(valid, rows[i], 1.0 if i in (0, 3, 5) else 0.0) for i in range(6)]
    inverse = [jnp.where(valid, x, 0.0) for x in symmetric_inverse(diag)]
    return diag, rows, inverse


def sweeps(diag, rows, inverse, rhs):
    update = [damping * x for x in sym_apply(inverse, rhs)]
    for _ in range(1, ITERS_ATT):
        applied = sym_apply(diag, update)
        for offset in range(1, 4):
            upper = rows[6 * offset : 6 * offset + 6]
            ahead = [pltpu.roll(x, LANES - offset, 1) for x in update]
            behind = [pltpu.roll(x, offset, 1) for x in sym_apply(upper, update)]
            for at, x in enumerate(sym_apply(upper, ahead)):
                applied[at] = applied[at] + x + behind[at]
        step = sym_apply(inverse, [rhs[at] - applied[at] for at in range(3)])
        update = [update[at] + damping * step[at] for at in range(3)]
    return update


def block_slice(block, width):
    return pl.ds(pl.multiple_of(block * width, 128), width)


def pair_sum(received, blocks, first):
    def step(number, total):
        return total + received[first, number]

    return lax.fori_loop(1, blocks, step, received[first, 0])


def update_kernel(
    n_src, n_seg, knots, halo,
    res_in, ow_in, tf_in, sp_in, ad_in, osrc_in, oint_in, prior_in, att_in, cnt,
    out_upd, out_att, out_res,
    res, ow, tf, sp, ad, osrc, oint, prior, att_prior,
    acc, sums, got_sums, upd, norm, got_norm, rhs, got_rhs, window, finals,
    hot_lo, hot_knot, spline, corr,
    in_sem, sum_send, sum_recv, upd_send, upd_recv, norm_send, norm_recv,
    rhs_send, rhs_recv, fin_send, fin_recv,
):
    count = n_src * n_seg
    src = lax.axis_index("src")
    seg = lax.axis_index("seg")
    me = src * n_seg + seg
    width = res.shape[1] // n_src
    groups = upd.shape[0]
    share = groups // n_seg

    loads = [
        pltpu.make_async_copy(a, b, in_sem.at[number])
        for number, (a, b) in enumerate(
            [(osrc_in, osrc), (ow_in, ow), (sp_in, sp), (res_in, res), (oint_in, oint),
             (tf_in, tf), (ad_in, ad), (att_in, att_prior), (prior_in, prior)]
        )
    ]
    for load in loads:
        load.start()

    barrier = pltpu.get_barrier_semaphore()

    def greet(number, carry):
        other = lax.rem(me + number, count)
        pl.semaphore_signal(
            barrier, inc=1, device_id=(lax.div(other, n_seg), lax.rem(other, n_seg)),
            device_id_type=pl.DeviceIdType.MESH,
        )
        return carry

    lax.fori_loop(1, count, greet, 0)

    def remote(a, b, send, recv, to_src, to_seg):
        return pltpu.make_async_remote_copy(
            src_ref=a, dst_ref=b, send_sem=send, recv_sem=recv,
            device_id=(to_src, to_seg), device_id_type=pl.DeviceIdType.MESH,
        )

    acc[...] = jnp.zeros_like(acc)
    for load in loads[:4]:
        load.wait()

    def source_step(block, carry):
        sl = block_slice(block, width)
        source = osrc[:, sl]
        hot = one_hot(source % LO, LO)
        hot_lo[block] = hot
        weight = live_weight(ow[:, sl], cnt[0, block])
        split = source_sums_block(sp[:, sl], weight, res[:, sl], source, hot)
        acc[...] += contract_lanes(expand(split, source // LO, groups), hot)
        return carry

    lax.fori_loop(0, n_src, source_step, 0)
    for group in range(groups):
        sums[group] = acc[48 * group : 48 * group + 24] + acc[48 * group + 24 : 48 * group + 48]

    pl.semaphore_wait(barrier, count - 1)

    def sum_copy(step):
        to = lax.rem(seg + step, n_seg)
        return remote(sums.at[pl.ds(to * share, share)], got_sums.at[step - 1],
                      sum_send.at[step - 1], sum_recv.at[step - 1], src, to)

    for step in range(1, n_seg):
        sum_copy(step).start()

    for load in loads[4:]:
        load.wait()

    def knot_copy(buffer, got, send, recv, block, delta):
        to = lax.rem(block * n_seg + seg + delta + count, count)
        return remote(buffer.at[block], got.at[delta + 1, src], send.at[delta + 1, block],
                      recv.at[delta + 1, src], lax.div(to, n_seg), lax.rem(to, n_seg))

    def knot_send(buffer, got, send, recv, number, block):
        knot_copy(buffer, got, send, recv, block, -1).start()
        knot_copy(buffer, got, send, recv, block, 1).start()

        @pl.when(number > 0)
        def _():
            knot_copy(buffer, got, send, recv, block, 0).start()

        @pl.when(number == 0)
        def _():
            got[1, src] = buffer[src]

    def knot_wait(buffer, got, send, recv):
        def step(number, carry):
            other = lax.rem(src + number, n_src)
            for delta in (-1, 0, 1):
                copy = remote(buffer.at[other], got.at[delta + 1, other],
                              send.at[delta + 1, other], recv.at[delta + 1, other], src, seg)
                if delta == 0:
                    pl.when(number > 0)(copy.wait_recv)
                else:
                    copy.wait_recv()
            return carry

        lax.fori_loop(0, n_src, step, 0)

    def knot_sent(buffer, got, send, recv):
        def step(number, carry):
            block = lax.rem(src + number, n_src)
            for delta in (-1, 0, 1):
                copy = knot_copy(buffer, got, send, recv, block, delta)
                if delta == 0:
                    pl.when(number > 0)(copy.wait_send)
                else:
                    copy.wait_send()
            return carry

        lax.fori_loop(0, n_src, step, 0)

    norm_set = (norm, got_norm, norm_send, norm_recv)
    rhs_set = (rhs, got_rhs, rhs_send, rhs_recv)

    blank = jnp.zeros((3, LANES - knots), F32)
    prior_ext = pltpu.roll(
        jnp.concatenate(
            [jnp.concatenate([att_prior[...], blank], 1), jnp.zeros((5, LANES), F32)], 0
        ), 1, 1,
    )
    zero1 = jnp.zeros((1, LANES), F32)
    zero2 = jnp.zeros((2, LANES), F32)
    prior_rows = jnp.concatenate(
        [prior_ext[0:1], zero2, prior_ext[1:2], zero1, prior_ext[2:3],
         jnp.zeros((18, LANES), F32)], 0
    )

    def normal_step(number, carry):
        block = lax.rem(src + number, n_src)
        sl = block_slice(block, width)
        weight = live_weight(ow[:, sl], cnt[0, block])
        floor_at, splines = basis(oint[:, sl], tf[:, sl], knots)
        hot = one_hot(floor_at, LANES)
        hot_knot[block] = hot
        spline[block] = jnp.concatenate(splines, 0)
        first = jnp.where(number == 0, 1.0, 0.0)
        norm[block] = normal_block(ad[:, sl], weight, splines, hot) + first * prior_rows
        knot_send(*norm_set, number, block)
        return carry

    lax.fori_loop(0, n_src, normal_step, 0)

    for step in range(1, n_seg):
        sum_copy(step).wait_recv()
    for group in range(share):
        total = sums[seg * share + group]
        for step in range(1, n_seg):
            total = total + got_sums[step - 1, group]
        start = pl.multiple_of((seg * share + group) * LO, LO)
        upd[seg * share + group] = cholesky_solve5(total, prior[:, pl.ds(start, LO)])

    def upd_copy(step, owner):
        part = upd.at[pl.ds(owner * share, share)]
        return remote(part, part, upd_send.at[step - 1], upd_recv.at[step - 1],
                      src, lax.rem(seg + step, n_seg))

    for step in range(1, n_seg):
        upd_copy(step, seg).start()

    knot_wait(*norm_set)
    valid = knot_valid(me, halo, knots, count * knots)
    normals = window_of(pair_sum(got_norm, n_src, 2), pair_sum(got_norm, n_src, 1),
                        pair_sum(got_norm, n_src, 0), halo, knots, me, count)
    diag, rows, inverse = prepare(normals, valid)
    window[...] = jnp.concatenate(diag + rows[6:] + inverse + [zero2], 0)

    for step in range(1, n_seg):
        upd_copy(step, lax.rem(seg - step + n_seg, n_seg)).wait_recv()
    for group in range(groups):
        out_upd[:, group * LO : (group + 1) * LO] = upd[group, :5]
    table = split_rows(jnp.concatenate([upd[group] for group in range(groups)], 0))

    def first_step(number, carry):
        block = lax.rem(src + number, n_src)
        sl = block_slice(block, width)
        weight = live_weight(ow[:, sl], cnt[0, block])
        found = source_lookup(table, hot_lo[block], osrc[:, sl] // LO, sp[:, sl])
        corr[:, sl] = found
        splines = [spline[block, at : at + 1] for at in range(4)]
        rhs[block] = rhs_block(
            ad[:, sl], weight * (res[:, sl] - found), splines, hot_knot[block]
        )
        knot_send(*rhs_set, number, block)
        return carry

    lax.fori_loop(0, n_src, first_step, 0)

    knot_wait(*rhs_set)
    right = window_of(pair_sum(got_rhs, n_src, 2), pair_sum(got_rhs, n_src, 1),
                      pair_sum(got_rhs, n_src, 0), halo, knots, me, count)
    right = [jnp.where(valid, right[at : at + 1], 0.0) for at in range(3)]
    rows = [window[at : at + 1] for at in range(24)]
    inverse = [window[at : at + 1] for at in range(24, 30)]
    update = sweeps(rows[:6], rows, inverse, right)
    final = jnp.concatenate(update + [jnp.zeros((5, LANES), F32)], 0)
    finals[src] = final
    out_att[...] = pltpu.roll(final, LANES - halo, 1)[:3, :knots]

    def fin_copy(number, owner):
        return remote(finals.at[owner], finals.at[owner], fin_send.at[number],
                      fin_recv.at[number], lax.rem(src + number, n_src), seg)

    def fin_start(number, carry):
        fin_copy(number, src).start()
        return carry

    lax.fori_loop(1, n_src, fin_start, 0)

    def last_step(number, carry):
        block = lax.rem(src - number + n_src, n_src)
        sl = block_slice(block, width)

        @pl.when(number > 0)
        def _():
            fin_copy(number, block).wait_recv()

        splines = [spline[block, at : at + 1] for at in range(4)]
        att = attitude_lookup(finals[block], halo - 1, hot_knot[block], splines, ad[:, sl])
        out_res[:, sl] = res[:, sl] - live_weight(corr[:, sl] + att, cnt[0, block])
        return carry

    lax.fori_loop(0, n_src, last_step, 0)

    def fin_sent(number, carry):
        fin_copy(number, src).wait_send()
        return carry

    lax.fori_loop(1, n_src, fin_sent, 0)
    for step in range(1, n_seg):
        sum_copy(step).wait_send()
        upd_copy(step, seg).wait_send()
    knot_sent(*norm_set)
    knot_sent(*rhs_set)


def body(residual, obs_weight, time_frac, src_partials, att_dir, src_prior, att_prior,
         obs_source, obs_interval, obs_count):
    n_src = lax.axis_size("src")
    n_seg = lax.axis_size("seg")
    obs = residual.shape[0]
    sources = src_prior.shape[1]
    knots = att_prior.shape[1]
    groups = sources // LO
    share = groups // n_seg
    width = obs // n_src
    row = lambda x: x.reshape(1, obs)
    ints = pltpu.VMEM((1, obs), jnp.int32)
    line = pltpu.VMEM((1, obs), F32)
    dma = pltpu.SemaphoreType.DMA
    anywhere = pl.BlockSpec(memory_space=pl.ANY)
    src_update, att_update, out = pl.pallas_call(
        functools.partial(update_kernel, n_src, n_seg, knots, 32),
        out_shape=[jax.ShapeDtypeStruct(shape, F32)
                   for shape in ((5, sources), (3, knots), (1, obs))],
        in_specs=[anywhere] * 9 + [smem],
        out_specs=[vmem] * 3,
        scratch_shapes=[
            line, line, line, pltpu.VMEM((5, obs), F32), pltpu.VMEM((3, obs), F32), ints, ints,
            pltpu.VMEM((5, sources), F32), pltpu.VMEM((3, knots), F32),
            pltpu.VMEM((groups * 48, LO), F32),
            pltpu.VMEM((groups, 24, LO), F32),
            pltpu.VMEM((n_seg - 1, share, 24, LO), F32),
            pltpu.VMEM((groups, 8, LO), F32),
            pltpu.VMEM((n_src, 24, LANES), F32),
            pltpu.VMEM((3, n_src, 24, LANES), F32),
            pltpu.VMEM((n_src, 8, LANES), F32),
            pltpu.VMEM((3, n_src, 8, LANES), F32),
            pltpu.VMEM((32, LANES), F32),
            pltpu.VMEM((n_src, 8, LANES), F32),
            pltpu.VMEM((n_src, LO, width), BF16),
            pltpu.VMEM((n_src, LANES, width), BF16),
            pltpu.VMEM((n_src, 4, width), F32),
            line,
            dma((9,)), dma((n_seg - 1,)), dma((n_seg - 1,)), dma((n_seg - 1,)), dma((n_seg - 1,)),
            dma((3, n_src)), dma((3, n_src)), dma((3, n_src)), dma((3, n_src)),
            dma((n_src,)), dma((n_src,)),
        ],
        compiler_params=pltpu.CompilerParams(
            collective_id=0, has_side_effects=True, vmem_limit_bytes=56 * 2**20
        ),
    )(row(residual), row(obs_weight), row(time_frac), src_partials, att_dir, row(obs_source),
      row(obs_interval), src_prior, att_prior, obs_count)
    return src_update, att_update, out.reshape(obs)


def solution(mesh):
    both = P(("src", "seg"))
    wide = P(None, ("src", "seg"))
    in_specs = (both, both, both, wide, wide, P(None, "src"), wide, both, both,
                P(("src", "seg"), None))
    out_specs = (P(None, "src"), wide, both)
    return jax.shard_map(body, mesh=mesh, in_specs=in_specs, out_specs=out_specs, check_vma=False)
```

```python
import functools

import jax
import jax.numpy as jnp
from jax import lax
from jax.experimental import pallas as pl
from jax.experimental.pallas import tpu as pltpu
from jax.sharding import PartitionSpec as P

ITERS_ATT = 6
LO = 256
LO_BITS = 8
SIXTH = 1.0 / 6.0
LANES = 128
F32 = jnp.float32
BF16 = jnp.bfloat16
PAIR_ROW = {}
for _d in range(3):
    for _p in range(5):
        _q = (_p + _d) % 5
        PAIR_ROW[_p, _q] = 5 * _d + _p
        PAIR_ROW[_q, _p] = 5 * _d + _p
damping = 0.5
vmem = pl.BlockSpec(memory_space=pltpu.VMEM)
smem = pl.BlockSpec(memory_space=pltpu.SMEM)


def split_rows(values):
    high = values.astype(BF16).astype(F32)
    return jnp.concatenate([high, values - high], 0).astype(BF16)


def contract_lanes(left, right):
    return lax.dot_general(left, right, (((1,), (1,)), ((), ())), preferred_element_type=F32)


def matmul(left, right):
    return lax.dot_general(left, right, (((1,), (0,)), ((), ())), preferred_element_type=F32)


def one_hot(index_row, rows):
    width = index_row.shape[1]
    ids = lax.broadcasted_iota(jnp.int32, (16, width), 0).astype(F32).astype(BF16)
    wanted = jnp.broadcast_to(index_row.astype(F32), (16, width)).astype(BF16)
    one = jnp.ones((16, width), BF16)
    zero = jnp.zeros((16, width), BF16)
    return jnp.concatenate(
        [jnp.where(wanted == ids + start, one, zero) for start in range(0, rows, 16)], 0
    )


def live_weight(weight_row, count):
    place = lax.broadcasted_iota(jnp.int32, weight_row.shape, 1)
    return jnp.where(place < count, weight_row, 0.0)


def basis(interval_row, frac_row, first):
    local_time = (interval_row - first).astype(F32) + frac_row
    floor_part = jnp.floor(local_time)
    u = local_time - floor_part
    square = u * u
    cube = square * u
    rest = 1.0 - u
    splines = [
        rest * rest * rest * SIXTH,
        (3.0 * cube - 6.0 * square + 4.0) * SIXTH,
        (-3.0 * cube + 3.0 * square + 3.0 * u + 1.0) * SIXTH,
        cube * SIXTH,
    ]
    return floor_part.astype(jnp.int32), splines


def source_sums_block(partials, weight, residual, source, hot):
    width = partials.shape[1]
    weighted = partials * weight
    features = jnp.concatenate(
        [
            weighted * partials,
            weighted * jnp.concatenate([partials[1:], partials[:1]], 0),
            weighted * jnp.concatenate([partials[2:], partials[:2]], 0),
            weighted * residual,
            jnp.zeros((4, width), F32),
        ],
        0,
    )
    return split_rows(features)


def expand(split, high_row, groups):
    width = split.shape[1]
    high16 = jnp.broadcast_to(high_row, (16, width))
    parts = []
    for group in range(groups):
        mask = jnp.where(high16 == group, 1.0, 0.0).astype(BF16)
        for start in range(0, split.shape[0], 16):
            parts.append(split[start : start + 16] * mask)
    return jnp.concatenate(parts, 0)


def normal_block(direction, weight, splines, hot):
    blank = jnp.zeros((2, direction.shape[1]), F32)
    d0, d1, d2 = direction[0:1], direction[1:2], direction[2:3]
    entries = (
        weight
        * jnp.concatenate([d0, d0, d0, d1, d1, d2, blank], 0)
        * jnp.concatenate([d0, d1, d2, d1, d2, d2, blank], 0)
    )
    groups = []
    for at in range(4):
        for offset in range(4 - at):
            groups.append((splines[at] * splines[at + offset]) * entries)
    rows = 8 * len(groups)
    sums = contract_lanes(split_rows(jnp.concatenate(groups, 0)), hot)
    sums = sums[:rows] + sums[rows:]
    upper = [None] * 4
    number = 0
    for at in range(4):
        for offset in range(4 - at):
            term = sums[8 * number : 8 * number + 8]
            term = term if at == 0 else pltpu.roll(term, at, 1)
            upper[offset] = term if upper[offset] is None else upper[offset] + term
            number += 1
    return jnp.concatenate([term[:6] for term in upper], 0)


def rhs_block(direction, weighted_first, splines, hot):
    base = jnp.concatenate(
        [direction * weighted_first, jnp.zeros((5, direction.shape[1]), F32)], 0
    )
    sums = contract_lanes(split_rows(jnp.concatenate([s * base for s in splines], 0)), hot)
    sums = sums[:32] + sums[32:]
    total = sums[:8]
    for at in range(1, 4):
        total = total + pltpu.roll(sums[8 * at : 8 * at + 8], at, 1)
    return total


def cholesky_solve5(sums, prior):
    factor = {}
    inverse = [None] * 5
    for row in range(5):
        for col in range(row + 1):
            at = PAIR_ROW[row, col]
            running = sums[at : at + 1]
            if row == col:
                running = running + prior[row : row + 1]
            for k in range(col):
                running = running - factor[row, k] * factor[col, k]
            if row == col:
                inverse[row] = 1.0 / jnp.sqrt(running)
            else:
                factor[row, col] = running * inverse[col]
    forward = []
    for row in range(5):
        running = sums[15 + row : 16 + row]
        for k in range(row):
            running = running - factor[row, k] * forward[k]
        forward.append(running * inverse[row])
    backward = [None] * 5
    for row in reversed(range(5)):
        running = forward[row]
        for k in range(row + 1, 5):
            running = running - factor[k, row] * backward[k]
        backward[row] = running * inverse[row]
    return jnp.concatenate(backward + [jnp.zeros((3, LO), F32)], 0)


def source_lookup(table, hot, high_row, partials):
    groups = table.shape[0] // 16
    looked = matmul(table, hot)
    half = 8 * groups
    high8 = jnp.broadcast_to(high_row, (8, hot.shape[1]))
    chosen = None
    for group in range(groups):
        term = looked[8 * group : 8 * group + 8] + looked[half + 8 * group : half + 8 * group + 8]
        term = jnp.where(high8 == group, term, 0.0)
        chosen = term if chosen is None else chosen + term
    return jnp.sum(partials * chosen[:5], 0, keepdims=True)


def attitude_lookup(window, shift, hot, splines, direction):
    tables = [pltpu.roll(window, LANES - (shift + at), 1) for at in range(4)]
    looked = matmul(split_rows(jnp.concatenate(tables, 0)), hot)
    looked = looked[:32] + looked[32:]
    total = None
    for at in range(4):
        term = splines[at] * looked[8 * at : 8 * at + 3]
        total = term if total is None else total + term
    return jnp.sum(direction * total, 0, keepdims=True)


def sym_apply(e, v):
    return [
        e[0] * v[0] + e[1] * v[1] + e[2] * v[2],
        e[1] * v[0] + e[3] * v[1] + e[4] * v[2],
        e[2] * v[0] + e[4] * v[1] + e[5] * v[2],
    ]


def symmetric_inverse(e):
    c00 = e[3] * e[5] - e[4] * e[4]
    c01 = e[2] * e[4] - e[1] * e[5]
    c02 = e[1] * e[4] - e[2] * e[3]
    c11 = e[0] * e[5] - e[2] * e[2]
    c12 = e[1] * e[2] - e[0] * e[4]
    c22 = e[0] * e[3] - e[1] * e[1]
    det = e[0] * c00 + e[1] * c01 + e[2] * c02
    return [c / det for c in (c00, c01, c02, c11, c12, c22)]


def window_of(before, own, after, halo, knots, me, count):
    lane = lax.broadcasted_iota(jnp.int32, own.shape, 1)
    left = pltpu.roll(before, (halo - 1 - knots) % LANES, 1)
    right = pltpu.roll(after, (halo - 1 + knots) % LANES, 1)
    total = pltpu.roll(own, halo - 1, 1)
    total = total + jnp.where((lane < halo + 2) & (me > 0), left, 0.0)
    return total + jnp.where((lane >= halo - 1 + knots) & (me < count - 1), right, 0.0)


def knot_valid(me, halo, knots, total):
    lane = lax.broadcasted_iota(jnp.int32, (1, LANES), 1)
    knot = me * knots + lane - halo
    return (knot >= 0) & (knot < total)


def prepare(normals, valid):
    rows = [jnp.where(valid, normals[i : i + 1], 0.0) for i in range(24)]
    diag = [jnp.where(valid, rows[i], 1.0 if i in (0, 3, 5) else 0.0) for i in range(6)]
    inverse = [jnp.where(valid, x, 0.0) for x in symmetric_inverse(diag)]
    return diag, rows, inverse


def sweeps(diag, rows, inverse, rhs):
    update = [damping * x for x in sym_apply(inverse, rhs)]
    for _ in range(1, ITERS_ATT):
        applied = sym_apply(diag, update)
        for offset in range(1, 4):
            upper = rows[6 * offset : 6 * offset + 6]
            ahead = [pltpu.roll(x, LANES - offset, 1) for x in update]
            behind = [pltpu.roll(x, offset, 1) for x in sym_apply(upper, update)]
            for at, x in enumerate(sym_apply(upper, ahead)):
                applied[at] = applied[at] + x + behind[at]
        step = sym_apply(inverse, [rhs[at] - applied[at] for at in range(3)])
        update = [update[at] + damping * step[at] for at in range(3)]
    return update


def block_slice(block, width):
    return pl.ds(pl.multiple_of(block * width, 128), width)


def pair_sum(received, blocks, first):
    def step(number, total):
        return total + received[first, number]

    return lax.fori_loop(1, blocks, step, received[first, 0])


def update_kernel(
    n_src, n_seg, knots, halo,
    res_in, ow_in, tf_in, sp_in, ad_in, osrc_in, oint_in, prior_in, att_in, cnt,
    out_upd, out_att, out_res,
    res, ow, tf, sp, ad, osrc, oint, prior, att_prior,
    acc, sums, got_sums, upd, norm, got_norm, own_norm, beside, rhs, got_rhs, finals,
    hot_lo, hot_knot, spline, corr,
    in_sem, sum_send, sum_recv, upd_send, upd_recv, norm_send, norm_recv, beside_send, beside_recv,
    rhs_send, rhs_recv, fin_send, fin_recv,
):
    count = n_src * n_seg
    src = lax.axis_index("src")
    seg = lax.axis_index("seg")
    me = src * n_seg + seg
    width = res.shape[1] // n_src
    groups = upd.shape[0]
    share = groups // n_seg

    loads = [
        pltpu.make_async_copy(a, b, in_sem.at[number])
        for number, (a, b) in enumerate(
            [(osrc_in, osrc), (ow_in, ow), (sp_in, sp), (res_in, res), (oint_in, oint),
             (tf_in, tf), (ad_in, ad), (att_in, att_prior), (prior_in, prior)]
        )
    ]
    for load in loads:
        load.start()

    barrier = pltpu.get_barrier_semaphore()

    def greet(number, carry):
        other = lax.rem(me + number, count)
        pl.semaphore_signal(
            barrier, inc=1, device_id=(lax.div(other, n_seg), lax.rem(other, n_seg)),
            device_id_type=pl.DeviceIdType.MESH,
        )
        return carry

    lax.fori_loop(1, count, greet, 0)

    def remote(a, b, send, recv, to_src, to_seg):
        return pltpu.make_async_remote_copy(
            src_ref=a, dst_ref=b, send_sem=send, recv_sem=recv,
            device_id=(to_src, to_seg), device_id_type=pl.DeviceIdType.MESH,
        )

    acc[...] = jnp.zeros_like(acc)
    for load in loads[:4]:
        load.wait()

    def source_step(block, carry):
        sl = block_slice(block, width)
        source = osrc[:, sl]
        hot = one_hot(source & (LO - 1), LO)
        hot_lo[block] = hot
        weight = live_weight(ow[:, sl], cnt[0, block])
        split = source_sums_block(sp[:, sl], weight, res[:, sl], source, hot)
        acc[...] += contract_lanes(expand(split, source >> LO_BITS, groups), hot)
        return carry

    lax.fori_loop(0, n_src, source_step, 0)
    for group in range(groups):
        sums[group] = acc[48 * group : 48 * group + 24] + acc[48 * group + 24 : 48 * group + 48]

    pl.semaphore_wait(barrier, count - 1)

    def sum_copy(step):
        to = lax.rem(seg + step, n_seg)
        return remote(sums.at[pl.ds(to * share, share)], got_sums.at[step - 1],
                      sum_send.at[step - 1], sum_recv.at[step - 1], src, to)

    for step in range(1, n_seg):
        sum_copy(step).start()

    for load in loads[4:]:
        load.wait()

    def knot_copy(buffer, got, send, recv, block, delta):
        to = lax.rem(block * n_seg + seg + delta + count, count)
        return remote(buffer.at[block], got.at[delta + 1, src], send.at[delta + 1, block],
                      recv.at[delta + 1, src], lax.div(to, n_seg), lax.rem(to, n_seg))

    def knot_send(buffer, got, send, recv, number, block):
        knot_copy(buffer, got, send, recv, block, -1).start()
        knot_copy(buffer, got, send, recv, block, 1).start()

        @pl.when(number > 0)
        def _():
            knot_copy(buffer, got, send, recv, block, 0).start()

        @pl.when(number == 0)
        def _():
            got[1, src] = buffer[src]

    def knot_wait(buffer, got, send, recv):
        def step(number, carry):
            other = lax.rem(src + number, n_src)
            for delta in (-1, 0, 1):
                copy = remote(buffer.at[other], got.at[delta + 1, other],
                              send.at[delta + 1, other], recv.at[delta + 1, other], src, seg)
                if delta == 0:
                    pl.when(number > 0)(copy.wait_recv)
                else:
                    copy.wait_recv()
            return carry

        lax.fori_loop(0, n_src, step, 0)

    def knot_sent(buffer, got, send, recv):
        def step(number, carry):
            block = lax.rem(src + number, n_src)
            for delta in (-1, 0, 1):
                copy = knot_copy(buffer, got, send, recv, block, delta)
                if delta == 0:
                    pl.when(number > 0)(copy.wait_send)
                else:
                    copy.wait_send()
            return carry

        lax.fori_loop(0, n_src, step, 0)

    def norm_copy(number, block):
        return remote(norm.at[block], got_norm.at[number - 1], norm_send.at[number - 1],
                      norm_recv.at[number - 1], block, seg)

    def beside_copy(slot):
        to = lax.rem(me + (1 if slot == 0 else count - 1), count)
        return remote(own_norm, beside.at[slot], beside_send.at[slot], beside_recv.at[slot],
                      lax.div(to, n_seg), lax.rem(to, n_seg))

    rhs_set = (rhs, got_rhs, rhs_send, rhs_recv)

    blank = jnp.zeros((3, LANES - knots), F32)
    prior_ext = pltpu.roll(
        jnp.concatenate(
            [jnp.concatenate([att_prior[...], blank], 1), jnp.zeros((5, LANES), F32)], 0
        ), 1, 1,
    )
    zero1 = jnp.zeros((1, LANES), F32)
    zero2 = jnp.zeros((2, LANES), F32)
    prior_rows = jnp.concatenate(
        [prior_ext[0:1], zero2, prior_ext[1:2], zero1, prior_ext[2:3],
         jnp.zeros((18, LANES), F32)], 0
    )

    def normal_step(number, carry):
        block = lax.rem(src + number, n_src)
        sl = block_slice(block, width)
        weight = live_weight(ow[:, sl], cnt[0, block])
        floor_at, splines = basis(oint[:, sl], tf[:, sl], (block * n_seg + seg) * knots)
        hot = one_hot(floor_at, LANES)
        hot_knot[block] = hot
        spline[block] = jnp.concatenate(splines, 0)
        norm[block] = normal_block(ad[:, sl], weight, splines, hot)

        @pl.when(number > 0)
        def _():
            norm_copy(number, block).start()

        return carry

    lax.fori_loop(0, n_src, normal_step, 0)

    for step in range(1, n_seg):
        sum_copy(step).wait_recv()
    for group in range(share):
        total = sums[seg * share + group]
        for step in range(1, n_seg):
            total = total + got_sums[step - 1, group]
        start = pl.multiple_of((seg * share + group) * LO, LO)
        upd[seg * share + group] = cholesky_solve5(total, prior[:, pl.ds(start, LO)])

    def upd_copy(step, owner):
        part = upd.at[pl.ds(owner * share, share)]
        return remote(part, part, upd_send.at[step - 1], upd_recv.at[step - 1],
                      src, lax.rem(seg + step, n_seg))

    for step in range(1, n_seg):
        upd_copy(step, seg).start()

    def norm_sum(number, total):
        norm_copy(number, src).wait_recv()
        return total + got_norm[number - 1]

    own_norm[...] = lax.fori_loop(1, n_src, norm_sum, norm[src] + prior_rows)
    for slot in range(2):
        beside_copy(slot).start()

    for step in range(1, n_seg):
        upd_copy(step, lax.rem(seg - step + n_seg, n_seg)).wait_recv()
    for group in range(groups):
        out_upd[:, group * LO : (group + 1) * LO] = upd[group, :5]
    table = split_rows(jnp.concatenate([upd[group] for group in range(groups)], 0))

    def first_step(number, carry):
        block = lax.rem(src + number, n_src)
        sl = block_slice(block, width)
        weight = live_weight(ow[:, sl], cnt[0, block])
        found = source_lookup(table, hot_lo[block], osrc[:, sl] >> LO_BITS, sp[:, sl])
        corr[:, sl] = found
        splines = [spline[block, at : at + 1] for at in range(4)]
        rhs[block] = rhs_block(
            ad[:, sl], weight * (res[:, sl] - found), splines, hot_knot[block]
        )
        knot_send(*rhs_set, number, block)
        return carry

    lax.fori_loop(0, n_src, first_step, 0)

    for slot in range(2):
        beside_copy(slot).wait_recv()
    valid = knot_valid(me, halo, knots, count * knots)
    normals = window_of(beside[0], own_norm[...], beside[1], halo, knots, me, count)
    diag, rows, inverse = prepare(normals, valid)

    knot_wait(*rhs_set)
    right = window_of(pair_sum(got_rhs, n_src, 2), pair_sum(got_rhs, n_src, 1),
                      pair_sum(got_rhs, n_src, 0), halo, knots, me, count)
    right = [jnp.where(valid, right[at : at + 1], 0.0) for at in range(3)]
    update = sweeps(diag, rows, inverse, right)
    final = jnp.concatenate(update + [jnp.zeros((5, LANES), F32)], 0)
    finals[src] = final
    out_att[...] = pltpu.roll(final, LANES - halo, 1)[:3, :knots]

    def fin_copy(number, owner):
        return remote(finals.at[owner], finals.at[owner], fin_send.at[number],
                      fin_recv.at[number], lax.rem(src + number, n_src), seg)

    def fin_start(number, carry):
        fin_copy(number, src).start()
        return carry

    lax.fori_loop(1, n_src, fin_start, 0)

    def last_step(number, carry):
        block = lax.rem(src - number + n_src, n_src)
        sl = block_slice(block, width)

        @pl.when(number > 0)
        def _():
            fin_copy(number, block).wait_recv()

        splines = [spline[block, at : at + 1] for at in range(4)]
        att = attitude_lookup(finals[block], halo - 1, hot_knot[block], splines, ad[:, sl])
        out_res[:, sl] = res[:, sl] - live_weight(corr[:, sl] + att, cnt[0, block])
        return carry

    lax.fori_loop(0, n_src, last_step, 0)

    def fin_sent(number, carry):
        fin_copy(number, src).wait_send()
        return carry

    lax.fori_loop(1, n_src, fin_sent, 0)
    for step in range(1, n_seg):
        sum_copy(step).wait_send()
        upd_copy(step, seg).wait_send()
    for slot in range(2):
        beside_copy(slot).wait_send()

    def norm_sent(number, carry):
        norm_copy(number, lax.rem(src + number, n_src)).wait_send()
        return carry

    lax.fori_loop(1, n_src, norm_sent, 0)
    knot_sent(*rhs_set)


def body(residual, obs_weight, time_frac, src_partials, att_dir, src_prior, att_prior,
         obs_source, obs_interval, obs_count):
    n_src = lax.axis_size("src")
    n_seg = lax.axis_size("seg")
    obs = residual.shape[0]
    sources = src_prior.shape[1]
    knots = att_prior.shape[1]
    groups = sources // LO
    share = groups // n_seg
    width = obs // n_src
    row = lambda x: x.reshape(1, obs)
    ints = pltpu.VMEM((1, obs), jnp.int32)
    line = pltpu.VMEM((1, obs), F32)
    dma = pltpu.SemaphoreType.DMA
    anywhere = pl.BlockSpec(memory_space=pl.ANY)
    src_update, att_update, out = pl.pallas_call(
        functools.partial(update_kernel, n_src, n_seg, knots, 32),
        out_shape=[jax.ShapeDtypeStruct(shape, F32)
                   for shape in ((5, sources), (3, knots), (1, obs))],
        in_specs=[anywhere] * 9 + [smem],
        out_specs=[vmem] * 3,
        scratch_shapes=[
            line, line, line, pltpu.VMEM((5, obs), F32), pltpu.VMEM((3, obs), F32), ints, ints,
            pltpu.VMEM((5, sources), F32), pltpu.VMEM((3, knots), F32),
            pltpu.VMEM((groups * 48, LO), F32),
            pltpu.VMEM((groups, 24, LO), F32),
            pltpu.VMEM((n_seg - 1, share, 24, LO), F32),
            pltpu.VMEM((groups, 8, LO), F32),
            pltpu.VMEM((n_src, 24, LANES), F32),
            pltpu.VMEM((n_src - 1, 24, LANES), F32),
            pltpu.VMEM((24, LANES), F32),
            pltpu.VMEM((2, 24, LANES), F32),
            pltpu.VMEM((n_src, 8, LANES), F32),
            pltpu.VMEM((3, n_src, 8, LANES), F32),
            pltpu.VMEM((n_src, 8, LANES), F32),
            pltpu.VMEM((n_src, LO, width), BF16),
            pltpu.VMEM((n_src, LANES, width), BF16),
            pltpu.VMEM((n_src, 4, width), F32),
            line,
            dma((9,)), dma((n_seg - 1,)), dma((n_seg - 1,)), dma((n_seg - 1,)), dma((n_seg - 1,)),
            dma((n_src - 1,)), dma((n_src - 1,)), dma((2,)), dma((2,)),
            dma((3, n_src)), dma((3, n_src)),
            dma((n_src,)), dma((n_src,)),
        ],
        compiler_params=pltpu.CompilerParams(
            collective_id=0, has_side_effects=True, vmem_limit_bytes=56 * 2**20
        ),
    )(row(residual), row(obs_weight), row(time_frac), src_partials, att_dir, row(obs_source),
      row(obs_interval), src_prior, att_prior, obs_count)
    return src_update, att_update, out.reshape(obs)


def solution(mesh):
    both = P(("src", "seg"))
    wide = P(None, ("src", "seg"))
    in_specs = (both, both, both, wide, wide, P(None, "src"), wide, both, both,
                P(("src", "seg"), None))
    out_specs = (P(None, "src"), wide, both)
    return jax.shard_map(body, mesh=mesh, in_specs=in_specs, out_specs=out_specs, check_vma=False)
```

```python
import functools

import jax
import jax.numpy as jnp
from jax import lax
from jax.experimental import pallas as pl
from jax.experimental.pallas import tpu as pltpu
from jax.sharding import PartitionSpec as P

ITERS_ATT = 6
LO = 256
LO_BITS = 8
SIXTH = 1.0 / 6.0
LANES = 128
F32 = jnp.float32
BF16 = jnp.bfloat16
PAIR_ROW = {}
for _d in range(3):
    for _p in range(5):
        _q = (_p + _d) % 5
        PAIR_ROW[_p, _q] = 5 * _d + _p
        PAIR_ROW[_q, _p] = 5 * _d + _p
damping = 0.5
vmem = pl.BlockSpec(memory_space=pltpu.VMEM)
smem = pl.BlockSpec(memory_space=pltpu.SMEM)


def split_rows(values):
    high = values.astype(BF16).astype(F32)
    return jnp.concatenate([high, values - high], 0).astype(BF16)


def contract_lanes(left, right):
    return lax.dot_general(left, right, (((1,), (1,)), ((), ())), preferred_element_type=F32)


def matmul(left, right):
    return lax.dot_general(left, right, (((1,), (0,)), ((), ())), preferred_element_type=F32)


def one_hot(index_row, rows):
    width = index_row.shape[1]
    ids = lax.broadcasted_iota(jnp.int32, (16, width), 0).astype(F32).astype(BF16)
    wanted = jnp.broadcast_to(index_row.astype(F32), (16, width)).astype(BF16)
    one = jnp.ones((16, width), BF16)
    zero = jnp.zeros((16, width), BF16)
    return jnp.concatenate(
        [jnp.where(wanted == ids + start, one, zero) for start in range(0, rows, 16)], 0
    )


def live_weight(weight_row, count):
    place = lax.broadcasted_iota(jnp.int32, weight_row.shape, 1)
    return jnp.where(place < count, weight_row, 0.0)


def basis(interval_row, frac_row, first):
    local_time = (interval_row - first).astype(F32) + frac_row
    floor_part = jnp.floor(local_time)
    u = local_time - floor_part
    square = u * u
    cube = square * u
    rest = 1.0 - u
    splines = [
        rest * rest * rest * SIXTH,
        (3.0 * cube - 6.0 * square + 4.0) * SIXTH,
        (-3.0 * cube + 3.0 * square + 3.0 * u + 1.0) * SIXTH,
        cube * SIXTH,
    ]
    return floor_part.astype(jnp.int32), splines


def source_sums_block(partials, weight, residual, source, hot):
    width = partials.shape[1]
    weighted = partials * weight
    features = jnp.concatenate(
        [
            weighted * partials,
            weighted * jnp.concatenate([partials[1:], partials[:1]], 0),
            weighted * jnp.concatenate([partials[2:], partials[:2]], 0),
            weighted * residual,
            jnp.zeros((4, width), F32),
        ],
        0,
    )
    return split_rows(features)


def expand(split, high_row, groups):
    width = split.shape[1]
    high16 = jnp.broadcast_to(high_row.astype(F32), (16, width)).astype(BF16)
    zero = jnp.zeros((16, width), BF16)
    parts = []
    for group in range(groups):
        mask = high16 == jnp.full((16, width), group, BF16)
        for start in range(0, split.shape[0], 16):
            parts.append(jnp.where(mask, split[start : start + 16], zero))
    return jnp.concatenate(parts, 0)


def normal_block(direction, weight, splines, hot):
    blank = jnp.zeros((2, direction.shape[1]), F32)
    d0, d1, d2 = direction[0:1], direction[1:2], direction[2:3]
    entries = (
        weight
        * jnp.concatenate([d0, d0, d0, d1, d1, d2, blank], 0)
        * jnp.concatenate([d0, d1, d2, d1, d2, d2, blank], 0)
    )
    groups = []
    for at in range(4):
        for offset in range(4 - at):
            groups.append((splines[at] * splines[at + offset]) * entries)
    rows = 8 * len(groups)
    sums = contract_lanes(split_rows(jnp.concatenate(groups, 0)), hot)
    sums = sums[:rows] + sums[rows:]
    upper = [None] * 4
    number = 0
    for at in range(4):
        for offset in range(4 - at):
            term = sums[8 * number : 8 * number + 8]
            term = term if at == 0 else pltpu.roll(term, at, 1)
            upper[offset] = term if upper[offset] is None else upper[offset] + term
            number += 1
    return jnp.concatenate([term[:6] for term in upper], 0)


def rhs_block(direction, weighted_first, splines, hot):
    base = jnp.concatenate(
        [direction * weighted_first, jnp.zeros((5, direction.shape[1]), F32)], 0
    )
    sums = contract_lanes(split_rows(jnp.concatenate([s * base for s in splines], 0)), hot)
    sums = sums[:32] + sums[32:]
    total = sums[:8]
    for at in range(1, 4):
        total = total + pltpu.roll(sums[8 * at : 8 * at + 8], at, 1)
    return total


def cholesky_solve5(sums, prior):
    factor = {}
    inverse = [None] * 5
    for row in range(5):
        for col in range(row + 1):
            at = PAIR_ROW[row, col]
            running = sums[at : at + 1]
            if row == col:
                running = running + prior[row : row + 1]
            for k in range(col):
                running = running - factor[row, k] * factor[col, k]
            if row == col:
                inverse[row] = 1.0 / jnp.sqrt(running)
            else:
                factor[row, col] = running * inverse[col]
    forward = []
    for row in range(5):
        running = sums[15 + row : 16 + row]
        for k in range(row):
            running = running - factor[row, k] * forward[k]
        forward.append(running * inverse[row])
    backward = [None] * 5
    for row in reversed(range(5)):
        running = forward[row]
        for k in range(row + 1, 5):
            running = running - factor[k, row] * backward[k]
        backward[row] = running * inverse[row]
    return jnp.concatenate(backward + [jnp.zeros((3, LO), F32)], 0)


def source_lookup(table, hot, high_row, partials):
    groups = table.shape[0] // 16
    looked = matmul(table, hot)
    half = 8 * groups
    high8 = jnp.broadcast_to(high_row, (8, hot.shape[1]))
    chosen = None
    for group in range(groups):
        term = looked[8 * group : 8 * group + 8] + looked[half + 8 * group : half + 8 * group + 8]
        term = jnp.where(high8 == group, term, 0.0)
        chosen = term if chosen is None else chosen + term
    return jnp.sum(partials * chosen[:5], 0, keepdims=True)


def attitude_lookup(window, shift, hot, splines, direction):
    tables = [pltpu.roll(window, LANES - (shift + at), 1) for at in range(4)]
    looked = matmul(split_rows(jnp.concatenate(tables, 0)), hot)
    looked = looked[:32] + looked[32:]
    total = None
    for at in range(4):
        term = splines[at] * looked[8 * at : 8 * at + 3]
        total = term if total is None else total + term
    return jnp.sum(direction * total, 0, keepdims=True)


def sym_apply(e, v):
    return [
        e[0] * v[0] + e[1] * v[1] + e[2] * v[2],
        e[1] * v[0] + e[3] * v[1] + e[4] * v[2],
        e[2] * v[0] + e[4] * v[1] + e[5] * v[2],
    ]


def symmetric_inverse(e):
    c00 = e[3] * e[5] - e[4] * e[4]
    c01 = e[2] * e[4] - e[1] * e[5]
    c02 = e[1] * e[4] - e[2] * e[3]
    c11 = e[0] * e[5] - e[2] * e[2]
    c12 = e[1] * e[2] - e[0] * e[4]
    c22 = e[0] * e[3] - e[1] * e[1]
    det = e[0] * c00 + e[1] * c01 + e[2] * c02
    return [c / det for c in (c00, c01, c02, c11, c12, c22)]


def window_of(before, own, after, halo, knots, me, count):
    lane = lax.broadcasted_iota(jnp.int32, own.shape, 1)
    left = pltpu.roll(before, (halo - 1 - knots) % LANES, 1)
    right = pltpu.roll(after, (halo - 1 + knots) % LANES, 1)
    total = pltpu.roll(own, halo - 1, 1)
    total = total + jnp.where((lane < halo + 2) & (me > 0), left, 0.0)
    return total + jnp.where((lane >= halo - 1 + knots) & (me < count - 1), right, 0.0)


def knot_valid(me, halo, knots, total):
    lane = lax.broadcasted_iota(jnp.int32, (1, LANES), 1)
    knot = me * knots + lane - halo
    return (knot >= 0) & (knot < total)


def prepare(normals, valid):
    rows = [jnp.where(valid, normals[i : i + 1], 0.0) for i in range(24)]
    diag = [jnp.where(valid, rows[i], 1.0 if i in (0, 3, 5) else 0.0) for i in range(6)]
    inverse = [jnp.where(valid, x, 0.0) for x in symmetric_inverse(diag)]
    return diag, rows, inverse


def shift_back(rows):
    return [
        pltpu.roll(rows[6 * offset + at], offset, 1) for offset in range(1, 4) for at in range(6)
    ]


def sweeps(diag, rows, lower, inverse, rhs):
    update = [damping * x for x in sym_apply(inverse, rhs)]
    for _ in range(1, ITERS_ATT):
        applied = sym_apply(diag, update)
        for offset in range(1, 4):
            ahead = [pltpu.roll(x, LANES - offset, 1) for x in update]
            behind = [pltpu.roll(x, offset, 1) for x in update]
            upper_part = sym_apply(rows[6 * offset : 6 * offset + 6], ahead)
            lower_part = sym_apply(lower[6 * offset - 6 : 6 * offset], behind)
            for at in range(3):
                applied[at] = applied[at] + (upper_part[at] + lower_part[at])
        step = sym_apply(inverse, [rhs[at] - applied[at] for at in range(3)])
        update = [update[at] + damping * step[at] for at in range(3)]
    return update


def block_slice(block, width):
    return pl.ds(pl.multiple_of(block * width, 128), width)


def pair_sum(received, blocks, first):
    def step(number, total):
        return total + received[first, number]

    return lax.fori_loop(1, blocks, step, received[first, 0])


def update_kernel(
    n_src, n_seg, knots, halo,
    res_in, ow_in, tf_in, sp_in, ad_in, osrc_in, oint_in, prior_in, att_in, cnt,
    upd_to, att_to, res_to,
    out_upd, out_att, out_res,
    res, ow, tf, sp, ad, osrc, oint, prior, att_prior,
    acc, sums, got_sums, upd, norm, got_norm, own_norm, beside, rhs, got_rhs, finals,
    hot_lo, hot_knot, spline, corr,
    in_sem, out_sem, res_sem, sum_send, sum_recv, upd_send, upd_recv, norm_send, norm_recv, beside_send, beside_recv,
    rhs_send, rhs_recv, fin_send, fin_recv,
):
    count = n_src * n_seg
    src = lax.axis_index("src")
    seg = lax.axis_index("seg")
    me = src * n_seg + seg
    width = res.shape[1] // n_src
    groups = upd.shape[0]
    share = groups // n_seg

    loads = [
        pltpu.make_async_copy(a, b, in_sem.at[number])
        for number, (a, b) in enumerate(
            [(osrc_in, osrc), (ow_in, ow), (sp_in, sp), (res_in, res), (oint_in, oint),
             (tf_in, tf), (ad_in, ad), (att_in, att_prior), (prior_in, prior)]
        )
    ]
    for load in loads:
        load.start()

    barrier = pltpu.get_barrier_semaphore()

    def greet(number, carry):
        other = lax.rem(me + number, count)
        pl.semaphore_signal(
            barrier, inc=1, device_id=(lax.div(other, n_seg), lax.rem(other, n_seg)),
            device_id_type=pl.DeviceIdType.MESH,
        )
        return carry

    lax.fori_loop(1, count, greet, 0)

    def remote(a, b, send, recv, to_src, to_seg):
        return pltpu.make_async_remote_copy(
            src_ref=a, dst_ref=b, send_sem=send, recv_sem=recv,
            device_id=(to_src, to_seg), device_id_type=pl.DeviceIdType.MESH,
        )

    acc[...] = jnp.zeros_like(acc)
    for load in loads[:4]:
        load.wait()

    def source_step(block, carry):
        sl = block_slice(block, width)
        source = osrc[:, sl]
        hot = one_hot(source & (LO - 1), LO)
        hot_lo[block] = hot
        weight = live_weight(ow[:, sl], cnt[0, block])
        split = source_sums_block(sp[:, sl], weight, res[:, sl], source, hot)
        acc[...] += contract_lanes(expand(split, source >> LO_BITS, groups), hot)
        return carry

    lax.fori_loop(0, n_src, source_step, 0)
    for group in range(groups):
        sums[group] = acc[48 * group : 48 * group + 24] + acc[48 * group + 24 : 48 * group + 48]

    pl.semaphore_wait(barrier, count - 1)

    def sum_copy(step):
        to = lax.rem(seg + step, n_seg)
        return remote(sums.at[pl.ds(to * share, share)], got_sums.at[step - 1],
                      sum_send.at[step - 1], sum_recv.at[step - 1], src, to)

    for step in range(1, n_seg):
        sum_copy(step).start()

    for load in loads[4:]:
        load.wait()

    def knot_copy(buffer, got, send, recv, block, delta):
        to = lax.rem(block * n_seg + seg + delta + count, count)
        return remote(buffer.at[block], got.at[delta + 1, src], send.at[delta + 1, block],
                      recv.at[delta + 1, src], lax.div(to, n_seg), lax.rem(to, n_seg))

    def knot_send(buffer, got, send, recv, number, block):
        knot_copy(buffer, got, send, recv, block, -1).start()
        knot_copy(buffer, got, send, recv, block, 1).start()

        @pl.when(number > 0)
        def _():
            knot_copy(buffer, got, send, recv, block, 0).start()

        @pl.when(number == 0)
        def _():
            got[1, src] = buffer[src]

    def knot_wait(buffer, got, send, recv):
        def step(number, carry):
            other = lax.rem(src + number, n_src)
            for delta in (-1, 0, 1):
                copy = remote(buffer.at[other], got.at[delta + 1, other],
                              send.at[delta + 1, other], recv.at[delta + 1, other], src, seg)
                if delta == 0:
                    pl.when(number > 0)(copy.wait_recv)
                else:
                    copy.wait_recv()
            return carry

        lax.fori_loop(0, n_src, step, 0)

    def knot_sent(buffer, got, send, recv):
        def step(number, carry):
            block = lax.rem(src + number, n_src)
            for delta in (-1, 0, 1):
                copy = knot_copy(buffer, got, send, recv, block, delta)
                if delta == 0:
                    pl.when(number > 0)(copy.wait_send)
                else:
                    copy.wait_send()
            return carry

        lax.fori_loop(0, n_src, step, 0)

    def norm_copy(number, block):
        return remote(norm.at[block], got_norm.at[number - 1], norm_send.at[number - 1],
                      norm_recv.at[number - 1], block, seg)

    def beside_copy(slot):
        to = lax.rem(me + (1 if slot == 0 else count - 1), count)
        return remote(own_norm, beside.at[slot], beside_send.at[slot], beside_recv.at[slot],
                      lax.div(to, n_seg), lax.rem(to, n_seg))

    rhs_set = (rhs, got_rhs, rhs_send, rhs_recv)

    blank = jnp.zeros((3, LANES - knots), F32)
    prior_ext = pltpu.roll(
        jnp.concatenate(
            [jnp.concatenate([att_prior[...], blank], 1), jnp.zeros((5, LANES), F32)], 0
        ), 1, 1,
    )
    zero1 = jnp.zeros((1, LANES), F32)
    zero2 = jnp.zeros((2, LANES), F32)
    prior_rows = jnp.concatenate(
        [prior_ext[0:1], zero2, prior_ext[1:2], zero1, prior_ext[2:3],
         jnp.zeros((18, LANES), F32)], 0
    )

    def normal_step(number, carry):
        block = lax.rem(src + number, n_src)
        sl = block_slice(block, width)
        weight = live_weight(ow[:, sl], cnt[0, block])
        floor_at, splines = basis(oint[:, sl], tf[:, sl], (block * n_seg + seg) * knots)
        hot = one_hot(floor_at, LANES)
        hot_knot[block] = hot
        spline[block] = jnp.concatenate(splines, 0)
        norm[block] = normal_block(ad[:, sl], weight, splines, hot)

        @pl.when(number > 0)
        def _():
            norm_copy(number, block).start()

        return carry

    lax.fori_loop(0, n_src, normal_step, 0)

    for step in range(1, n_seg):
        sum_copy(step).wait_recv()
    for group in range(share):
        total = sums[seg * share + group]
        for step in range(1, n_seg):
            total = total + got_sums[step - 1, group]
        start = pl.multiple_of((seg * share + group) * LO, LO)
        upd[seg * share + group] = cholesky_solve5(total, prior[:, pl.ds(start, LO)])

    def upd_copy(step, owner):
        part = upd.at[pl.ds(owner * share, share)]
        return remote(part, part, upd_send.at[step - 1], upd_recv.at[step - 1],
                      src, lax.rem(seg + step, n_seg))

    for step in range(1, n_seg):
        upd_copy(step, seg).start()

    def norm_sum(number, total):
        norm_copy(number, src).wait_recv()
        return total + got_norm[number - 1]

    own_norm[...] = lax.fori_loop(1, n_src, norm_sum, norm[src] + prior_rows)
    for slot in range(2):
        beside_copy(slot).start()

    for step in range(1, n_seg):
        upd_copy(step, lax.rem(seg - step + n_seg, n_seg)).wait_recv()
    for group in range(groups):
        out_upd[:, group * LO : (group + 1) * LO] = upd[group, :5]
    upd_store = pltpu.make_async_copy(out_upd, upd_to, out_sem.at[0])
    upd_store.start()
    table = split_rows(jnp.concatenate([upd[group] for group in range(groups)], 0))

    def first_step(number, carry):
        block = lax.rem(src + number, n_src)
        sl = block_slice(block, width)
        weight = live_weight(ow[:, sl], cnt[0, block])
        found = source_lookup(table, hot_lo[block], osrc[:, sl] >> LO_BITS, sp[:, sl])
        corr[:, sl] = found
        splines = [spline[block, at : at + 1] for at in range(4)]
        rhs[block] = rhs_block(
            ad[:, sl], weight * (res[:, sl] - found), splines, hot_knot[block]
        )[:4]
        knot_send(*rhs_set, number, block)
        return carry

    lax.fori_loop(0, n_src, first_step, 0)

    for slot in range(2):
        beside_copy(slot).wait_recv()
    valid = knot_valid(me, halo, knots, count * knots)
    normals = window_of(beside[0], own_norm[...], beside[1], halo, knots, me, count)
    diag, rows, inverse = prepare(normals, valid)
    lower = shift_back(rows)

    knot_wait(*rhs_set)
    right = window_of(pair_sum(got_rhs, n_src, 2), pair_sum(got_rhs, n_src, 1),
                      pair_sum(got_rhs, n_src, 0), halo, knots, me, count)
    right = [jnp.where(valid, right[at : at + 1], 0.0) for at in range(3)]
    update = sweeps(diag, rows, lower, inverse, right)
    final = jnp.concatenate(update + [jnp.zeros((5, LANES), F32)], 0)
    finals[src] = final

    def fin_copy(number, owner):
        return remote(finals.at[owner], finals.at[owner], fin_send.at[number],
                      fin_recv.at[number], lax.rem(src + number, n_src), seg)

    def fin_start(number, carry):
        fin_copy(number, src).start()
        return carry

    lax.fori_loop(1, n_src, fin_start, 0)

    out_att[...] = pltpu.roll(final, LANES - halo, 1)[:3, :knots]
    att_store = pltpu.make_async_copy(out_att, att_to, out_sem.at[1])
    att_store.start()

    def res_store(number, block):
        sl = block_slice(block, width)
        return pltpu.make_async_copy(out_res.at[:, sl], res_to.at[:, sl], res_sem.at[number])

    def last_step(number, carry):
        block = lax.rem(src - number + n_src, n_src)
        sl = block_slice(block, width)

        @pl.when(number > 0)
        def _():
            fin_copy(number, block).wait_recv()

        splines = [spline[block, at : at + 1] for at in range(4)]
        att = attitude_lookup(finals[block], halo - 1, hot_knot[block], splines, ad[:, sl])
        out_res[:, sl] = res[:, sl] - live_weight(corr[:, sl] + att, cnt[0, block])
        res_store(number, block).start()
        return carry

    lax.fori_loop(0, n_src, last_step, 0)

    def fin_sent(number, carry):
        fin_copy(number, src).wait_send()
        return carry

    lax.fori_loop(1, n_src, fin_sent, 0)
    for step in range(1, n_seg):
        sum_copy(step).wait_send()
        upd_copy(step, seg).wait_send()
    for slot in range(2):
        beside_copy(slot).wait_send()

    def norm_sent(number, carry):
        norm_copy(number, lax.rem(src + number, n_src)).wait_send()
        return carry

    lax.fori_loop(1, n_src, norm_sent, 0)
    knot_sent(*rhs_set)
    upd_store.wait()
    att_store.wait()

    def res_stored(number, carry):
        res_store(number, lax.rem(src - number + n_src, n_src)).wait()
        return carry

    lax.fori_loop(0, n_src, res_stored, 0)


def hand_over(a, b, c, a_to, b_to, c_to, sem):
    copies = [
        pltpu.make_async_copy(x, y, sem.at[number])
        for number, (x, y) in enumerate([(c, c_to), (a, a_to), (b, b_to)])
    ]
    for copy in copies:
        copy.start()
    for copy in copies:
        copy.wait()


def body(residual, obs_weight, time_frac, src_partials, att_dir, src_prior, att_prior,
         obs_source, obs_interval, obs_count):
    n_src = lax.axis_size("src")
    n_seg = lax.axis_size("seg")
    obs = residual.shape[0]
    sources = src_prior.shape[1]
    knots = att_prior.shape[1]
    groups = sources // LO
    share = groups // n_seg
    width = obs // n_src
    row = lambda x: x.reshape(1, obs)
    ints = pltpu.VMEM((1, obs), jnp.int32)
    line = pltpu.VMEM((1, obs), F32)
    dma = pltpu.SemaphoreType.DMA
    anywhere = pl.BlockSpec(memory_space=pl.ANY)
    outs = [jax.ShapeDtypeStruct(shape, F32) for shape in ((5, sources), (3, knots), (1, obs))]
    made = pl.pallas_call(
        functools.partial(update_kernel, n_src, n_seg, knots, 32),
        out_shape=outs,
        in_specs=[anywhere] * 9 + [smem],
        out_specs=[anywhere] * 3,
        scratch_shapes=[
            pltpu.VMEM((5, sources), F32), pltpu.VMEM((3, knots), F32), line,
            line, line, line, pltpu.VMEM((5, obs), F32), pltpu.VMEM((3, obs), F32), ints, ints,
            pltpu.VMEM((5, sources), F32), pltpu.VMEM((3, knots), F32),
            pltpu.VMEM((groups * 48, LO), F32),
            pltpu.VMEM((groups, 24, LO), F32),
            pltpu.VMEM((n_seg - 1, share, 24, LO), F32),
            pltpu.VMEM((groups, 8, LO), F32),
            pltpu.VMEM((n_src, 24, LANES), F32),
            pltpu.VMEM((n_src - 1, 24, LANES), F32),
            pltpu.VMEM((24, LANES), F32),
            pltpu.VMEM((2, 24, LANES), F32),
            pltpu.VMEM((n_src, 4, LANES), F32),
            pltpu.VMEM((3, n_src, 4, LANES), F32),
            pltpu.VMEM((n_src, 8, LANES), F32),
            pltpu.VMEM((n_src, LO, width), BF16),
            pltpu.VMEM((n_src, LANES, width), BF16),
            pltpu.VMEM((n_src, 4, width), F32),
            line,
            dma((9,)), dma((2,)), dma((n_src,)), dma((n_seg - 1,)), dma((n_seg - 1,)), dma((n_seg - 1,)), dma((n_seg - 1,)),
            dma((n_src - 1,)), dma((n_src - 1,)), dma((2,)), dma((2,)),
            dma((3, n_src)), dma((3, n_src)),
            dma((n_src,)), dma((n_src,)),
        ],
        compiler_params=pltpu.CompilerParams(
            collective_id=0, has_side_effects=True, vmem_limit_bytes=56 * 2**20
        ),
    )(row(residual), row(obs_weight), row(time_frac), src_partials, att_dir, row(obs_source),
      row(obs_interval), src_prior, att_prior, obs_count)
    src_update, att_update, out = pl.pallas_call(
        hand_over,
        out_shape=outs,
        in_specs=[anywhere] * 3,
        out_specs=[anywhere] * 3,
        scratch_shapes=[dma((3,))],
        compiler_params=pltpu.CompilerParams(vmem_limit_bytes=56 * 2**20),
    )(*made)
    return src_update, att_update, out.reshape(obs)


def solution(mesh):
    both = P(("src", "seg"))
    wide = P(None, ("src", "seg"))
    in_specs = (both, both, both, wide, wide, P(None, "src"), wide, both, both,
                P(("src", "seg"), None))
    out_specs = (P(None, "src"), wide, both)
    return jax.shard_map(body, mesh=mesh, in_specs=in_specs, out_specs=out_specs, check_vma=False)
```

```python
import functools

import jax
import jax.numpy as jnp
from jax import lax
from jax.experimental import pallas as pl
from jax.experimental.pallas import tpu as pltpu
from jax.sharding import PartitionSpec as P

ITERS_ATT = 6
LO = 256
LO_BITS = 8
SIXTH = 1.0 / 6.0
LANES = 128
F32 = jnp.float32
BF16 = jnp.bfloat16
PAIR_ROW = {}
for _d in range(3):
    for _p in range(5):
        _q = (_p + _d) % 5
        PAIR_ROW[_p, _q] = 5 * _d + _p
        PAIR_ROW[_q, _p] = 5 * _d + _p
damping = 0.5
vmem = pl.BlockSpec(memory_space=pltpu.VMEM)
smem = pl.BlockSpec(memory_space=pltpu.SMEM)


def split_rows(values):
    high = values.astype(BF16).astype(F32)
    return jnp.concatenate([high, values - high], 0).astype(BF16)


def contract_lanes(left, right):
    return lax.dot_general(left, right, (((1,), (1,)), ((), ())), preferred_element_type=F32)


def matmul(left, right):
    return lax.dot_general(left, right, (((1,), (0,)), ((), ())), preferred_element_type=F32)


def one_hot(index_row, rows):
    width = index_row.shape[1]
    ids = lax.broadcasted_iota(jnp.int32, (16, width), 0).astype(F32).astype(BF16)
    wanted = jnp.broadcast_to(index_row.astype(F32), (16, width)).astype(BF16)
    one = jnp.ones((16, width), BF16)
    zero = jnp.zeros((16, width), BF16)
    return jnp.concatenate(
        [jnp.where(wanted == ids + start, one, zero) for start in range(0, rows, 16)], 0
    )


def live_weight(weight_row, count):
    place = lax.broadcasted_iota(jnp.int32, weight_row.shape, 1)
    return jnp.where(place < count, weight_row, 0.0)


def basis(interval_row, frac_row, first):
    local_time = (interval_row - first).astype(F32) + frac_row
    floor_part = jnp.floor(local_time)
    u = local_time - floor_part
    square = u * u
    cube = square * u
    rest = 1.0 - u
    splines = [
        rest * rest * rest * SIXTH,
        (3.0 * cube - 6.0 * square + 4.0) * SIXTH,
        (-3.0 * cube + 3.0 * square + 3.0 * u + 1.0) * SIXTH,
        cube * SIXTH,
    ]
    return floor_part.astype(jnp.int32), splines


def source_sums_block(partials, weight, residual, source, hot):
    width = partials.shape[1]
    weighted = partials * weight
    features = jnp.concatenate(
        [
            weighted * partials,
            weighted * jnp.concatenate([partials[1:], partials[:1]], 0),
            weighted * jnp.concatenate([partials[2:], partials[:2]], 0),
            weighted * residual,
            jnp.zeros((4, width), F32),
        ],
        0,
    )
    return split_rows(features)


def expand(split, high_row, groups):
    width = split.shape[1]
    high16 = jnp.broadcast_to(high_row.astype(F32), (16, width)).astype(BF16)
    zero = jnp.zeros((16, width), BF16)
    parts = []
    for group in range(groups):
        mask = high16 == jnp.full((16, width), group, BF16)
        for start in range(0, split.shape[0], 16):
            parts.append(jnp.where(mask, split[start : start + 16], zero))
    return jnp.concatenate(parts, 0)


def normal_block(direction, weight, splines, hot):
    blank = jnp.zeros((2, direction.shape[1]), F32)
    d0, d1, d2 = direction[0:1], direction[1:2], direction[2:3]
    entries = (
        weight
        * jnp.concatenate([d0, d0, d0, d1, d1, d2, blank], 0)
        * jnp.concatenate([d0, d1, d2, d1, d2, d2, blank], 0)
    )
    groups = []
    for at in range(4):
        for offset in range(4 - at):
            groups.append((splines[at] * splines[at + offset]) * entries)
    rows = 8 * len(groups)
    sums = contract_lanes(split_rows(jnp.concatenate(groups, 0)), hot)
    sums = sums[:rows] + sums[rows:]
    upper = [None] * 4
    number = 0
    for at in range(4):
        for offset in range(4 - at):
            term = sums[8 * number : 8 * number + 8]
            term = term if at == 0 else pltpu.roll(term, at, 1)
            upper[offset] = term if upper[offset] is None else upper[offset] + term
            number += 1
    return jnp.concatenate([term[:6] for term in upper], 0)


def rhs_block(direction, weighted_first, splines, hot):
    base = jnp.concatenate(
        [direction * weighted_first, jnp.zeros((5, direction.shape[1]), F32)], 0
    )
    sums = contract_lanes(split_rows(jnp.concatenate([s * base for s in splines], 0)), hot)
    sums = sums[:32] + sums[32:]
    total = sums[:8]
    for at in range(1, 4):
        total = total + pltpu.roll(sums[8 * at : 8 * at + 8], at, 1)
    return total


def cholesky_solve5(sums, prior):
    factor = {}
    inverse = [None] * 5
    for row in range(5):
        for col in range(row + 1):
            at = PAIR_ROW[row, col]
            running = sums[at : at + 1]
            if row == col:
                running = running + prior[row : row + 1]
            for k in range(col):
                running = running - factor[row, k] * factor[col, k]
            if row == col:
                inverse[row] = 1.0 / jnp.sqrt(running)
            else:
                factor[row, col] = running * inverse[col]
    forward = []
    for row in range(5):
        running = sums[15 + row : 16 + row]
        for k in range(row):
            running = running - factor[row, k] * forward[k]
        forward.append(running * inverse[row])
    backward = [None] * 5
    for row in reversed(range(5)):
        running = forward[row]
        for k in range(row + 1, 5):
            running = running - factor[k, row] * backward[k]
        backward[row] = running * inverse[row]
    return jnp.concatenate(backward + [jnp.zeros((3, LO), F32)], 0)


def source_lookup(table, hot, high_row, partials):
    groups = table.shape[0] // 16
    looked = matmul(table, hot)
    half = 8 * groups
    high8 = jnp.broadcast_to(high_row, (8, hot.shape[1]))
    chosen = None
    for group in range(groups):
        term = looked[8 * group : 8 * group + 8] + looked[half + 8 * group : half + 8 * group + 8]
        term = jnp.where(high8 == group, term, 0.0)
        chosen = term if chosen is None else chosen + term
    return jnp.sum(partials * chosen[:5], 0, keepdims=True)


def attitude_lookup(window, shift, hot, splines, direction):
    tables = [pltpu.roll(window, LANES - (shift + at), 1) for at in range(4)]
    looked = matmul(split_rows(jnp.concatenate(tables, 0)), hot)
    looked = looked[:32] + looked[32:]
    total = None
    for at in range(4):
        term = splines[at] * looked[8 * at : 8 * at + 3]
        total = term if total is None else total + term
    return jnp.sum(direction * total, 0, keepdims=True)


def sym_apply(e, v):
    return [
        e[0] * v[0] + e[1] * v[1] + e[2] * v[2],
        e[1] * v[0] + e[3] * v[1] + e[4] * v[2],
        e[2] * v[0] + e[4] * v[1] + e[5] * v[2],
    ]


def symmetric_inverse(e):
    c00 = e[3] * e[5] - e[4] * e[4]
    c01 = e[2] * e[4] - e[1] * e[5]
    c02 = e[1] * e[4] - e[2] * e[3]
    c11 = e[0] * e[5] - e[2] * e[2]
    c12 = e[1] * e[2] - e[0] * e[4]
    c22 = e[0] * e[3] - e[1] * e[1]
    det = e[0] * c00 + e[1] * c01 + e[2] * c02
    return [c / det for c in (c00, c01, c02, c11, c12, c22)]


def window_of(before, own, after, halo, knots, me, count):
    lane = lax.broadcasted_iota(jnp.int32, own.shape, 1)
    left = pltpu.roll(before, (halo - 1 - knots) % LANES, 1)
    right = pltpu.roll(after, (halo - 1 + knots) % LANES, 1)
    total = pltpu.roll(own, halo - 1, 1)
    total = total + jnp.where((lane < halo + 2) & (me > 0), left, 0.0)
    return total + jnp.where((lane >= halo - 1 + knots) & (me < count - 1), right, 0.0)


def knot_valid(me, halo, knots, total):
    lane = lax.broadcasted_iota(jnp.int32, (1, LANES), 1)
    knot = me * knots + lane - halo
    return (knot >= 0) & (knot < total)


def prepare(normals, valid):
    rows = [jnp.where(valid, normals[i : i + 1], 0.0) for i in range(24)]
    diag = [jnp.where(valid, rows[i], 1.0 if i in (0, 3, 5) else 0.0) for i in range(6)]
    inverse = [jnp.where(valid, x, 0.0) for x in symmetric_inverse(diag)]
    return diag, rows, inverse


def shift_back(rows):
    return [
        pltpu.roll(rows[6 * offset + at], offset, 1) for offset in range(1, 4) for at in range(6)
    ]


def sweeps(diag, rows, lower, inverse, rhs):
    update = [damping * x for x in sym_apply(inverse, rhs)]
    for _ in range(1, ITERS_ATT):
        applied = sym_apply(diag, update)
        for offset in range(1, 4):
            ahead = [pltpu.roll(x, LANES - offset, 1) for x in update]
            behind = [pltpu.roll(x, offset, 1) for x in update]
            upper_part = sym_apply(rows[6 * offset : 6 * offset + 6], ahead)
            lower_part = sym_apply(lower[6 * offset - 6 : 6 * offset], behind)
            for at in range(3):
                applied[at] = applied[at] + (upper_part[at] + lower_part[at])
        step = sym_apply(inverse, [rhs[at] - applied[at] for at in range(3)])
        update = [update[at] + damping * step[at] for at in range(3)]
    return update


def block_slice(block, width):
    return pl.ds(pl.multiple_of(block * width, 128), width)


def pair_sum(received, blocks, first):
    def step(number, total):
        return total + received[first, number]

    return lax.fori_loop(1, blocks, step, received[first, 0])


def update_kernel(
    n_src, n_seg, knots, halo,
    res_in, ow_in, tf_in, sp_in, ad_in, osrc_in, oint_in, prior_in, att_in, cnt,
    upd_to, att_to, res_to,
    out_upd, out_att, out_res,
    res, ow, tf, sp, ad, osrc, oint, prior, att_prior,
    acc, sums, got_sums, upd, norm, got_norm, own_norm, beside, rhs, got_rhs, finals,
    hot_lo, hot_knot, spline, corr,
    in_sem, out_sem, res_sem, sum_send, sum_recv, upd_send, upd_recv, norm_send, norm_recv, beside_send, beside_recv,
    rhs_send, rhs_recv, fin_send, fin_recv,
):
    count = n_src * n_seg
    src = lax.axis_index("src")
    seg = lax.axis_index("seg")
    me = src * n_seg + seg
    width = res.shape[1] // n_src
    groups = upd.shape[0]
    share = groups // n_seg

    loads = [
        pltpu.make_async_copy(a, b, in_sem.at[number])
        for number, (a, b) in enumerate(
            [(osrc_in, osrc), (ow_in, ow), (sp_in, sp), (res_in, res), (oint_in, oint),
             (tf_in, tf), (ad_in, ad), (att_in, att_prior), (prior_in, prior)]
        )
    ]
    for load in loads:
        load.start()

    barrier = pltpu.get_barrier_semaphore()

    def greet(number, carry):
        other = lax.rem(me + number, count)
        pl.semaphore_signal(
            barrier, inc=1, device_id=(lax.div(other, n_seg), lax.rem(other, n_seg)),
            device_id_type=pl.DeviceIdType.MESH,
        )
        return carry

    lax.fori_loop(1, count, greet, 0)

    def remote(a, b, send, recv, to_src, to_seg):
        return pltpu.make_async_remote_copy(
            src_ref=a, dst_ref=b, send_sem=send, recv_sem=recv,
            device_id=(to_src, to_seg), device_id_type=pl.DeviceIdType.MESH,
        )

    acc[...] = jnp.zeros_like(acc)
    for load in loads[:4]:
        load.wait()

    def source_step(block, carry):
        sl = block_slice(block, width)
        source = osrc[:, sl]
        hot = one_hot(source & (LO - 1), LO)
        hot_lo[block] = hot
        weight = live_weight(ow[:, sl], cnt[0, block])
        split = source_sums_block(sp[:, sl], weight, res[:, sl], source, hot)
        acc[...] += contract_lanes(expand(split, source >> LO_BITS, groups), hot)
        return carry

    lax.fori_loop(0, n_src, source_step, 0, unroll=2)
    for group in range(groups):
        sums[group] = acc[48 * group : 48 * group + 24] + acc[48 * group + 24 : 48 * group + 48]

    pl.semaphore_wait(barrier, count - 1)

    def sum_copy(step):
        to = lax.rem(seg + step, n_seg)
        return remote(sums.at[pl.ds(to * share, share)], got_sums.at[step - 1],
                      sum_send.at[step - 1], sum_recv.at[step - 1], src, to)

    for step in range(1, n_seg):
        sum_copy(step).start()

    for load in loads[4:]:
        load.wait()

    def knot_copy(buffer, got, send, recv, block, delta):
        to = lax.rem(block * n_seg + seg + delta + count, count)
        return remote(buffer.at[block], got.at[delta + 1, src], send.at[delta + 1, block],
                      recv.at[delta + 1, src], lax.div(to, n_seg), lax.rem(to, n_seg))

    def knot_send(buffer, got, send, recv, number, block):
        knot_copy(buffer, got, send, recv, block, -1).start()
        knot_copy(buffer, got, send, recv, block, 1).start()

        @pl.when(number > 0)
        def _():
            knot_copy(buffer, got, send, recv, block, 0).start()

        @pl.when(number == 0)
        def _():
            got[1, src] = buffer[src]

    def knot_wait(buffer, got, send, recv):
        def step(number, carry):
            other = lax.rem(src + number, n_src)
            for delta in (-1, 0, 1):
                copy = remote(buffer.at[other], got.at[delta + 1, other],
                              send.at[delta + 1, other], recv.at[delta + 1, other], src, seg)
                if delta == 0:
                    pl.when(number > 0)(copy.wait_recv)
                else:
                    copy.wait_recv()
            return carry

        lax.fori_loop(0, n_src, step, 0)

    def knot_sent(buffer, got, send, recv):
        def step(number, carry):
            block = lax.rem(src + number, n_src)
            for delta in (-1, 0, 1):
                copy = knot_copy(buffer, got, send, recv, block, delta)
                if delta == 0:
                    pl.when(number > 0)(copy.wait_send)
                else:
                    copy.wait_send()
            return carry

        lax.fori_loop(0, n_src, step, 0)

    def norm_copy(number, block):
        return remote(norm.at[block], got_norm.at[number - 1], norm_send.at[number - 1],
                      norm_recv.at[number - 1], block, seg)

    def beside_copy(slot):
        to = lax.rem(me + (1 if slot == 0 else count - 1), count)
        return remote(own_norm, beside.at[slot], beside_send.at[slot], beside_recv.at[slot],
                      lax.div(to, n_seg), lax.rem(to, n_seg))

    rhs_set = (rhs, got_rhs, rhs_send, rhs_recv)

    blank = jnp.zeros((3, LANES - knots), F32)
    prior_ext = pltpu.roll(
        jnp.concatenate(
            [jnp.concatenate([att_prior[...], blank], 1), jnp.zeros((5, LANES), F32)], 0
        ), 1, 1,
    )
    zero1 = jnp.zeros((1, LANES), F32)
    zero2 = jnp.zeros((2, LANES), F32)
    prior_rows = jnp.concatenate(
        [prior_ext[0:1], zero2, prior_ext[1:2], zero1, prior_ext[2:3],
         jnp.zeros((18, LANES), F32)], 0
    )

    def normal_step(number, carry):
        block = lax.rem(src + number, n_src)
        sl = block_slice(block, width)
        weight = live_weight(ow[:, sl], cnt[0, block])
        floor_at, splines = basis(oint[:, sl], tf[:, sl], (block * n_seg + seg) * knots)
        hot = one_hot(floor_at, LANES)
        hot_knot[block] = hot
        spline[block] = jnp.concatenate(splines, 0)
        norm[block] = normal_block(ad[:, sl], weight, splines, hot)

        @pl.when(number > 0)
        def _():
            norm_copy(number, block).start()

        return carry

    lax.fori_loop(0, n_src, normal_step, 0)

    for step in range(1, n_seg):
        sum_copy(step).wait_recv()
    for group in range(share):
        total = sums[seg * share + group]
        for step in range(1, n_seg):
            total = total + got_sums[step - 1, group]
        start = pl.multiple_of((seg * share + group) * LO, LO)
        upd[seg * share + group] = cholesky_solve5(total, prior[:, pl.ds(start, LO)])

    def upd_copy(step, owner):
        part = upd.at[pl.ds(owner * share, share)]
        return remote(part, part, upd_send.at[step - 1], upd_recv.at[step - 1],
                      src, lax.rem(seg + step, n_seg))

    for step in range(1, n_seg):
        upd_copy(step, seg).start()

    def norm_sum(number, total):
        norm_copy(number, src).wait_recv()
        return total + got_norm[number - 1]

    own_norm[...] = lax.fori_loop(1, n_src, norm_sum, norm[src] + prior_rows)
    for slot in range(2):
        beside_copy(slot).start()

    for step in range(1, n_seg):
        upd_copy(step, lax.rem(seg - step + n_seg, n_seg)).wait_recv()
    for group in range(groups):
        out_upd[:, group * LO : (group + 1) * LO] = upd[group, :5]
    upd_store = pltpu.make_async_copy(out_upd, upd_to, out_sem.at[0])
    upd_store.start()
    table = split_rows(jnp.concatenate([upd[group] for group in range(groups)], 0))

    def first_step(number, carry):
        block = lax.rem(src + number, n_src)
        sl = block_slice(block, width)
        weight = live_weight(ow[:, sl], cnt[0, block])
        found = source_lookup(table, hot_lo[block], osrc[:, sl] >> LO_BITS, sp[:, sl])
        corr[:, sl] = found
        splines = [spline[block, at : at + 1] for at in range(4)]
        rhs[block] = rhs_block(
            ad[:, sl], weight * (res[:, sl] - found), splines, hot_knot[block]
        )[:4]
        knot_send(*rhs_set, number, block)
        return carry

    lax.fori_loop(0, n_src, first_step, 0)

    for slot in range(2):
        beside_copy(slot).wait_recv()
    valid = knot_valid(me, halo, knots, count * knots)
    normals = window_of(beside[0], own_norm[...], beside[1], halo, knots, me, count)
    diag, rows, inverse = prepare(normals, valid)
    lower = shift_back(rows)

    knot_wait(*rhs_set)
    right = window_of(pair_sum(got_rhs, n_src, 2), pair_sum(got_rhs, n_src, 1),
                      pair_sum(got_rhs, n_src, 0), halo, knots, me, count)
    right = [jnp.where(valid, right[at : at + 1], 0.0) for at in range(3)]
    update = sweeps(diag, rows, lower, inverse, right)
    final = jnp.concatenate(update + [jnp.zeros((5, LANES), F32)], 0)
    finals[src] = final

    def fin_copy(number, owner):
        return remote(finals.at[owner], finals.at[owner], fin_send.at[number],
                      fin_recv.at[number], lax.rem(src + number, n_src), seg)

    def fin_start(number, carry):
        fin_copy(number, src).start()
        return carry

    lax.fori_loop(1, n_src, fin_start, 0)

    out_att[...] = pltpu.roll(final, LANES - halo, 1)[:3, :knots]
    att_store = pltpu.make_async_copy(out_att, att_to, out_sem.at[1])
    att_store.start()

    def res_store(number, block):
        sl = block_slice(block, width)
        return pltpu.make_async_copy(out_res.at[:, sl], res_to.at[:, sl], res_sem.at[number])

    def last_step(number, carry):
        block = lax.rem(src - number + n_src, n_src)
        sl = block_slice(block, width)

        @pl.when(number > 0)
        def _():
            fin_copy(number, block).wait_recv()

        splines = [spline[block, at : at + 1] for at in range(4)]
        att = attitude_lookup(finals[block], halo - 1, hot_knot[block], splines, ad[:, sl])
        out_res[:, sl] = res[:, sl] - live_weight(corr[:, sl] + att, cnt[0, block])
        res_store(number, block).start()
        return carry

    lax.fori_loop(0, n_src, last_step, 0)

    def fin_sent(number, carry):
        fin_copy(number, src).wait_send()
        return carry

    lax.fori_loop(1, n_src, fin_sent, 0)
    for step in range(1, n_seg):
        sum_copy(step).wait_send()
        upd_copy(step, seg).wait_send()
    for slot in range(2):
        beside_copy(slot).wait_send()

    def norm_sent(number, carry):
        norm_copy(number, lax.rem(src + number, n_src)).wait_send()
        return carry

    lax.fori_loop(1, n_src, norm_sent, 0)
    knot_sent(*rhs_set)
    upd_store.wait()
    att_store.wait()

    def res_stored(number, carry):
        res_store(number, lax.rem(src - number + n_src, n_src)).wait()
        return carry

    lax.fori_loop(0, n_src, res_stored, 0)


def hand_over(a, b, c, a_to, b_to, c_to):
    a_to[...] = a[...]
    b_to[...] = b[...]
    c_to[...] = c[...]


def body(residual, obs_weight, time_frac, src_partials, att_dir, src_prior, att_prior,
         obs_source, obs_interval, obs_count):
    n_src = lax.axis_size("src")
    n_seg = lax.axis_size("seg")
    obs = residual.shape[0]
    sources = src_prior.shape[1]
    knots = att_prior.shape[1]
    groups = sources // LO
    share = groups // n_seg
    width = obs // n_src
    row = lambda x: x.reshape(1, obs)
    ints = pltpu.VMEM((1, obs), jnp.int32)
    line = pltpu.VMEM((1, obs), F32)
    dma = pltpu.SemaphoreType.DMA
    anywhere = pl.BlockSpec(memory_space=pl.ANY)
    outs = [jax.ShapeDtypeStruct(shape, F32) for shape in ((5, sources), (3, knots), (1, obs))]
    made = pl.pallas_call(
        functools.partial(update_kernel, n_src, n_seg, knots, 32),
        out_shape=outs,
        in_specs=[anywhere] * 9 + [smem],
        out_specs=[anywhere] * 3,
        scratch_shapes=[
            pltpu.VMEM((5, sources), F32), pltpu.VMEM((3, knots), F32), line,
            line, line, line, pltpu.VMEM((5, obs), F32), pltpu.VMEM((3, obs), F32), ints, ints,
            pltpu.VMEM((5, sources), F32), pltpu.VMEM((3, knots), F32),
            pltpu.VMEM((groups * 48, LO), F32),
            pltpu.VMEM((groups, 24, LO), F32),
            pltpu.VMEM((n_seg - 1, share, 24, LO), F32),
            pltpu.VMEM((groups, 8, LO), F32),
            pltpu.VMEM((n_src, 24, LANES), F32),
            pltpu.VMEM((n_src - 1, 24, LANES), F32),
            pltpu.VMEM((24, LANES), F32),
            pltpu.VMEM((2, 24, LANES), F32),
            pltpu.VMEM((n_src, 4, LANES), F32),
            pltpu.VMEM((3, n_src, 4, LANES), F32),
            pltpu.VMEM((n_src, 8, LANES), F32),
            pltpu.VMEM((n_src, LO, width), BF16),
            pltpu.VMEM((n_src, LANES, width), BF16),
            pltpu.VMEM((n_src, 4, width), F32),
            line,
            dma((9,)), dma((2,)), dma((n_src,)), dma((n_seg - 1,)), dma((n_seg - 1,)), dma((n_seg - 1,)), dma((n_seg - 1,)),
            dma((n_src - 1,)), dma((n_src - 1,)), dma((2,)), dma((2,)),
            dma((3, n_src)), dma((3, n_src)),
            dma((n_src,)), dma((n_src,)),
        ],
        compiler_params=pltpu.CompilerParams(
            collective_id=0, has_side_effects=True, vmem_limit_bytes=56 * 2**20
        ),
    )(row(residual), row(obs_weight), row(time_frac), src_partials, att_dir, row(obs_source),
      row(obs_interval), src_prior, att_prior, obs_count)
    src_update, att_update, out = pl.pallas_call(
        hand_over,
        out_shape=outs,
        in_specs=[vmem] * 3,
        out_specs=[vmem] * 3,
        compiler_params=pltpu.CompilerParams(vmem_limit_bytes=56 * 2**20),
    )(*made)
    return src_update, att_update, out.reshape(obs)


def solution(mesh):
    both = P(("src", "seg"))
    wide = P(None, ("src", "seg"))
    in_specs = (both, both, both, wide, wide, P(None, "src"), wide, both, both,
                P(("src", "seg"), None))
    out_specs = (P(None, "src"), wide, both)
    return jax.shard_map(body, mesh=mesh, in_specs=in_specs, out_specs=out_specs, check_vma=False)
```

```python
import functools

import jax
import jax.numpy as jnp
from jax import lax
from jax.experimental import pallas as pl
from jax.experimental.pallas import tpu as pltpu
from jax.sharding import PartitionSpec as P

ITERS_ATT = 6
LO = 256
LO_BITS = 8
SIXTH = 1.0 / 6.0
LANES = 128
F32 = jnp.float32
BF16 = jnp.bfloat16
PAIR_ROW = {}
for _d in range(3):
    for _p in range(5):
        _q = (_p + _d) % 5
        PAIR_ROW[_p, _q] = 5 * _d + _p
        PAIR_ROW[_q, _p] = 5 * _d + _p
damping = 0.5
vmem = pl.BlockSpec(memory_space=pltpu.VMEM)
smem = pl.BlockSpec(memory_space=pltpu.SMEM)


def split_rows(values):
    high = values.astype(BF16).astype(F32)
    return jnp.concatenate([high, values - high], 0).astype(BF16)


def contract_lanes(left, right):
    return lax.dot_general(left, right, (((1,), (1,)), ((), ())), preferred_element_type=F32)


def matmul(left, right):
    return lax.dot_general(left, right, (((1,), (0,)), ((), ())), preferred_element_type=F32)


def one_hot(index_row, rows):
    width = index_row.shape[1]
    ids = lax.broadcasted_iota(jnp.int32, (16, width), 0).astype(F32).astype(BF16)
    wanted = jnp.broadcast_to(index_row.astype(F32), (16, width)).astype(BF16)
    one = jnp.ones((16, width), BF16)
    zero = jnp.zeros((16, width), BF16)
    return jnp.concatenate(
        [jnp.where(wanted == ids + start, one, zero) for start in range(0, rows, 16)], 0
    )


def live_weight(weight_row, count):
    place = lax.broadcasted_iota(jnp.int32, weight_row.shape, 1)
    return jnp.where(place < count, weight_row, 0.0)


def basis(interval_row, frac_row, first):
    local_time = (interval_row - first).astype(F32) + frac_row
    floor_part = jnp.floor(local_time)
    u = local_time - floor_part
    square = u * u
    cube = square * u
    rest = 1.0 - u
    splines = [
        rest * rest * rest * SIXTH,
        (3.0 * cube - 6.0 * square + 4.0) * SIXTH,
        (-3.0 * cube + 3.0 * square + 3.0 * u + 1.0) * SIXTH,
        cube * SIXTH,
    ]
    return floor_part.astype(jnp.int32), splines


def source_sums_block(partials, weight, residual, source, hot):
    width = partials.shape[1]
    weighted = partials * weight
    features = jnp.concatenate(
        [
            weighted * partials,
            weighted * jnp.concatenate([partials[1:], partials[:1]], 0),
            weighted * jnp.concatenate([partials[2:], partials[:2]], 0),
            weighted * residual,
            jnp.zeros((4, width), F32),
        ],
        0,
    )
    return split_rows(features)


def expand(split, high_row, groups):
    width = split.shape[1]
    high16 = jnp.broadcast_to(high_row.astype(F32), (16, width)).astype(BF16)
    zero = jnp.zeros((16, width), BF16)
    parts = []
    for group in range(groups):
        mask = high16 == jnp.full((16, width), group, BF16)
        for start in range(0, split.shape[0], 16):
            parts.append(jnp.where(mask, split[start : start + 16], zero))
    return jnp.concatenate(parts, 0)


def normal_block(direction, weight, splines, hot):
    blank = jnp.zeros((2, direction.shape[1]), F32)
    d0, d1, d2 = direction[0:1], direction[1:2], direction[2:3]
    entries = (
        weight
        * jnp.concatenate([d0, d0, d0, d1, d1, d2, blank], 0)
        * jnp.concatenate([d0, d1, d2, d1, d2, d2, blank], 0)
    )
    groups = []
    for at in range(4):
        for offset in range(4 - at):
            groups.append((splines[at] * splines[at + offset]) * entries)
    rows = 8 * len(groups)
    sums = contract_lanes(split_rows(jnp.concatenate(groups, 0)), hot)
    sums = sums[:rows] + sums[rows:]
    upper = [None] * 4
    number = 0
    for at in range(4):
        for offset in range(4 - at):
            term = sums[8 * number : 8 * number + 8]
            term = term if at == 0 else pltpu.roll(term, at, 1)
            upper[offset] = term if upper[offset] is None else upper[offset] + term
            number += 1
    return jnp.concatenate([term[:6] for term in upper], 0)


def rhs_block(direction, weighted_first, splines, hot):
    base = jnp.concatenate(
        [direction * weighted_first, jnp.zeros((5, direction.shape[1]), F32)], 0
    )
    sums = contract_lanes(split_rows(jnp.concatenate([s * base for s in splines], 0)), hot)
    sums = sums[:32] + sums[32:]
    total = sums[:8]
    for at in range(1, 4):
        total = total + pltpu.roll(sums[8 * at : 8 * at + 8], at, 1)
    return total


def cholesky_solve5(sums, prior):
    factor = {}
    inverse = [None] * 5
    for row in range(5):
        for col in range(row + 1):
            at = PAIR_ROW[row, col]
            running = sums[at : at + 1]
            if row == col:
                running = running + prior[row : row + 1]
            for k in range(col):
                running = running - factor[row, k] * factor[col, k]
            if row == col:
                inverse[row] = 1.0 / jnp.sqrt(running)
            else:
                factor[row, col] = running * inverse[col]
    forward = []
    for row in range(5):
        running = sums[15 + row : 16 + row]
        for k in range(row):
            running = running - factor[row, k] * forward[k]
        forward.append(running * inverse[row])
    backward = [None] * 5
    for row in reversed(range(5)):
        running = forward[row]
        for k in range(row + 1, 5):
            running = running - factor[k, row] * backward[k]
        backward[row] = running * inverse[row]
    return jnp.concatenate(backward + [jnp.zeros((3, LO), F32)], 0)


def source_lookup(table, hot, high_row, partials):
    groups = table.shape[0] // 16
    looked = matmul(table, hot)
    half = 8 * groups
    high8 = jnp.broadcast_to(high_row, (8, hot.shape[1]))
    chosen = None
    for group in range(groups):
        term = looked[8 * group : 8 * group + 8] + looked[half + 8 * group : half + 8 * group + 8]
        term = jnp.where(high8 == group, term, 0.0)
        chosen = term if chosen is None else chosen + term
    return jnp.sum(partials * chosen[:5], 0, keepdims=True)


def attitude_lookup(window, shift, hot, splines, direction):
    tables = [pltpu.roll(window, LANES - (shift + at), 1) for at in range(4)]
    looked = matmul(split_rows(jnp.concatenate(tables, 0)), hot)
    looked = looked[:32] + looked[32:]
    total = None
    for at in range(4):
        term = splines[at] * looked[8 * at : 8 * at + 3]
        total = term if total is None else total + term
    return jnp.sum(direction * total, 0, keepdims=True)


def sym_apply(e, v):
    return [
        e[0] * v[0] + e[1] * v[1] + e[2] * v[2],
        e[1] * v[0] + e[3] * v[1] + e[4] * v[2],
        e[2] * v[0] + e[4] * v[1] + e[5] * v[2],
    ]


def symmetric_inverse(e):
    c00 = e[3] * e[5] - e[4] * e[4]
    c01 = e[2] * e[4] - e[1] * e[5]
    c02 = e[1] * e[4] - e[2] * e[3]
    c11 = e[0] * e[5] - e[2] * e[2]
    c12 = e[1] * e[2] - e[0] * e[4]
    c22 = e[0] * e[3] - e[1] * e[1]
    det = e[0] * c00 + e[1] * c01 + e[2] * c02
    return [c / det for c in (c00, c01, c02, c11, c12, c22)]


def window_of(before, own, after, halo, knots, me, count):
    lane = lax.broadcasted_iota(jnp.int32, own.shape, 1)
    left = pltpu.roll(before, (halo - 1 - knots) % LANES, 1)
    right = pltpu.roll(after, (halo - 1 + knots) % LANES, 1)
    total = pltpu.roll(own, halo - 1, 1)
    total = total + jnp.where((lane < halo + 2) & (me > 0), left, 0.0)
    return total + jnp.where((lane >= halo - 1 + knots) & (me < count - 1), right, 0.0)


def knot_valid(me, halo, knots, total):
    lane = lax.broadcasted_iota(jnp.int32, (1, LANES), 1)
    knot = me * knots + lane - halo
    return (knot >= 0) & (knot < total)


def prepare(normals, valid):
    rows = [jnp.where(valid, normals[i : i + 1], 0.0) for i in range(24)]
    diag = [jnp.where(valid, rows[i], 1.0 if i in (0, 3, 5) else 0.0) for i in range(6)]
    inverse = [jnp.where(valid, x, 0.0) for x in symmetric_inverse(diag)]
    return diag, rows, inverse


def shift_back(rows):
    return [
        pltpu.roll(rows[6 * offset + at], offset, 1) for offset in range(1, 4) for at in range(6)
    ]


def sweeps(diag, rows, lower, inverse, rhs):
    update = [damping * x for x in sym_apply(inverse, rhs)]
    for _ in range(1, ITERS_ATT):
        applied = sym_apply(diag, update)
        for offset in range(1, 4):
            ahead = [pltpu.roll(x, LANES - offset, 1) for x in update]
            behind = [pltpu.roll(x, offset, 1) for x in update]
            upper_part = sym_apply(rows[6 * offset : 6 * offset + 6], ahead)
            lower_part = sym_apply(lower[6 * offset - 6 : 6 * offset], behind)
            for at in range(3):
                applied[at] = applied[at] + (upper_part[at] + lower_part[at])
        step = sym_apply(inverse, [rhs[at] - applied[at] for at in range(3)])
        update = [update[at] + damping * step[at] for at in range(3)]
    return update


def block_slice(block, width):
    return pl.ds(pl.multiple_of(block * width, 128), width)


def pair_sum(received, blocks, first):
    def step(number, total):
        return total + received[first, number]

    return lax.fori_loop(1, blocks, step, received[first, 0])


def update_kernel(
    n_src, n_seg, knots, halo,
    res_in, ow_in, tf_in, sp_in, ad_in, osrc_in, oint_in, prior_in, att_in, cnt,
    upd_to, att_to, res_to,
    out_upd, out_att, out_res,
    res, ow, tf, sp, ad, osrc, oint, prior, att_prior,
    acc, sums, got_sums, upd, norm, got_norm, own_norm, beside, rhs, got_rhs, finals,
    hot_lo, hot_knot, spline, corr,
    in_sem, out_sem, res_sem, sum_send, sum_recv, upd_send, upd_recv, norm_send, norm_recv, beside_send, beside_recv,
    rhs_send, rhs_recv, fin_send, fin_recv,
):
    count = n_src * n_seg
    src = lax.axis_index("src")
    seg = lax.axis_index("seg")
    me = src * n_seg + seg
    width = res.shape[1] // n_src
    groups = upd.shape[0]
    share = groups // n_seg

    loads = [
        pltpu.make_async_copy(a, b, in_sem.at[number])
        for number, (a, b) in enumerate(
            [(osrc_in, osrc), (ow_in, ow), (sp_in, sp), (res_in, res), (oint_in, oint),
             (tf_in, tf), (ad_in, ad), (att_in, att_prior), (prior_in, prior)]
        )
    ]
    for load in loads:
        load.start()

    barrier = pltpu.get_barrier_semaphore()

    def greet(number, carry):
        other = lax.rem(me + number, count)
        pl.semaphore_signal(
            barrier, inc=1, device_id=(lax.div(other, n_seg), lax.rem(other, n_seg)),
            device_id_type=pl.DeviceIdType.MESH,
        )
        return carry

    lax.fori_loop(1, count, greet, 0)

    def remote(a, b, send, recv, to_src, to_seg):
        return pltpu.make_async_remote_copy(
            src_ref=a, dst_ref=b, send_sem=send, recv_sem=recv,
            device_id=(to_src, to_seg), device_id_type=pl.DeviceIdType.MESH,
        )

    acc[...] = jnp.zeros_like(acc)
    for load in loads[:4]:
        load.wait()

    def source_step(block, carry):
        sl = block_slice(block, width)
        source = osrc[:, sl]
        hot = one_hot(source & (LO - 1), LO)
        hot_lo[block] = hot
        weight = live_weight(ow[:, sl], cnt[0, block])
        split = source_sums_block(sp[:, sl], weight, res[:, sl], source, hot)
        acc[...] += contract_lanes(expand(split, source >> LO_BITS, groups), hot)
        return carry

    lax.fori_loop(0, n_src, source_step, 0, unroll=4)
    for group in range(groups):
        sums[group] = acc[48 * group : 48 * group + 24] + acc[48 * group + 24 : 48 * group + 48]

    pl.semaphore_wait(barrier, count - 1)

    def sum_copy(step):
        to = lax.rem(seg + step, n_seg)
        return remote(sums.at[pl.ds(to * share, share)], got_sums.at[step - 1],
                      sum_send.at[step - 1], sum_recv.at[step - 1], src, to)

    for step in range(1, n_seg):
        sum_copy(step).start()

    for load in loads[4:]:
        load.wait()

    def knot_copy(buffer, got, send, recv, block, delta):
        to = lax.rem(block * n_seg + seg + delta + count, count)
        return remote(buffer.at[block], got.at[delta + 1, src], send.at[delta + 1, block],
                      recv.at[delta + 1, src], lax.div(to, n_seg), lax.rem(to, n_seg))

    def knot_send(buffer, got, send, recv, number, block):
        knot_copy(buffer, got, send, recv, block, -1).start()
        knot_copy(buffer, got, send, recv, block, 1).start()

        @pl.when(number > 0)
        def _():
            knot_copy(buffer, got, send, recv, block, 0).start()

        @pl.when(number == 0)
        def _():
            got[1, src] = buffer[src]

    def knot_wait(buffer, got, send, recv):
        def step(number, carry):
            other = lax.rem(src + number, n_src)
            for delta in (-1, 0, 1):
                copy = remote(buffer.at[other], got.at[delta + 1, other],
                              send.at[delta + 1, other], recv.at[delta + 1, other], src, seg)
                if delta == 0:
                    pl.when(number > 0)(copy.wait_recv)
                else:
                    copy.wait_recv()
            return carry

        lax.fori_loop(0, n_src, step, 0)

    def knot_sent(buffer, got, send, recv):
        def step(number, carry):
            block = lax.rem(src + number, n_src)
            for delta in (-1, 0, 1):
                copy = knot_copy(buffer, got, send, recv, block, delta)
                if delta == 0:
                    pl.when(number > 0)(copy.wait_send)
                else:
                    copy.wait_send()
            return carry

        lax.fori_loop(0, n_src, step, 0)

    def norm_copy(number, block):
        return remote(norm.at[block], got_norm.at[number - 1], norm_send.at[number - 1],
                      norm_recv.at[number - 1], block, seg)

    def beside_copy(slot):
        to = lax.rem(me + (1 if slot == 0 else count - 1), count)
        return remote(own_norm, beside.at[slot], beside_send.at[slot], beside_recv.at[slot],
                      lax.div(to, n_seg), lax.rem(to, n_seg))

    rhs_set = (rhs, got_rhs, rhs_send, rhs_recv)

    blank = jnp.zeros((3, LANES - knots), F32)
    prior_ext = pltpu.roll(
        jnp.concatenate(
            [jnp.concatenate([att_prior[...], blank], 1), jnp.zeros((5, LANES), F32)], 0
        ), 1, 1,
    )
    zero1 = jnp.zeros((1, LANES), F32)
    zero2 = jnp.zeros((2, LANES), F32)
    prior_rows = jnp.concatenate(
        [prior_ext[0:1], zero2, prior_ext[1:2], zero1, prior_ext[2:3],
         jnp.zeros((18, LANES), F32)], 0
    )

    def normal_step(number, carry):
        block = lax.rem(src + number, n_src)
        sl = block_slice(block, width)
        weight = live_weight(ow[:, sl], cnt[0, block])
        floor_at, splines = basis(oint[:, sl], tf[:, sl], (block * n_seg + seg) * knots)
        hot = one_hot(floor_at, LANES)
        hot_knot[block] = hot
        spline[block] = jnp.concatenate(splines, 0)
        norm[block] = normal_block(ad[:, sl], weight, splines, hot)

        @pl.when(number > 0)
        def _():
            norm_copy(number, block).start()

        return carry

    lax.fori_loop(0, n_src, normal_step, 0)

    for step in range(1, n_seg):
        sum_copy(step).wait_recv()
    for group in range(share):
        total = sums[seg * share + group]
        for step in range(1, n_seg):
            total = total + got_sums[step - 1, group]
        start = pl.multiple_of((seg * share + group) * LO, LO)
        upd[seg * share + group] = cholesky_solve5(total, prior[:, pl.ds(start, LO)])

    def upd_copy(step, owner):
        part = upd.at[pl.ds(owner * share, share)]
        return remote(part, part, upd_send.at[step - 1], upd_recv.at[step - 1],
                      src, lax.rem(seg + step, n_seg))

    for step in range(1, n_seg):
        upd_copy(step, seg).start()

    def norm_sum(number, total):
        norm_copy(number, src).wait_recv()
        return total + got_norm[number - 1]

    own_norm[...] = lax.fori_loop(1, n_src, norm_sum, norm[src] + prior_rows)
    for slot in range(2):
        beside_copy(slot).start()

    for step in range(1, n_seg):
        upd_copy(step, lax.rem(seg - step + n_seg, n_seg)).wait_recv()
    for group in range(groups):
        out_upd[:, group * LO : (group + 1) * LO] = upd[group, :5]
    upd_store = pltpu.make_async_copy(out_upd, upd_to, out_sem.at[0])
    upd_store.start()
    table = split_rows(jnp.concatenate([upd[group] for group in range(groups)], 0))

    def first_step(number, carry):
        block = lax.rem(src + number, n_src)
        sl = block_slice(block, width)
        weight = live_weight(ow[:, sl], cnt[0, block])
        found = source_lookup(table, hot_lo[block], osrc[:, sl] >> LO_BITS, sp[:, sl])
        corr[:, sl] = found
        splines = [spline[block, at : at + 1] for at in range(4)]
        rhs[block] = rhs_block(
            ad[:, sl], weight * (res[:, sl] - found), splines, hot_knot[block]
        )[:4]
        knot_send(*rhs_set, number, block)
        return carry

    lax.fori_loop(0, n_src, first_step, 0)

    for slot in range(2):
        beside_copy(slot).wait_recv()
    valid = knot_valid(me, halo, knots, count * knots)
    normals = window_of(beside[0], own_norm[...], beside[1], halo, knots, me, count)
    diag, rows, inverse = prepare(normals, valid)
    lower = shift_back(rows)

    knot_wait(*rhs_set)
    right = window_of(pair_sum(got_rhs, n_src, 2), pair_sum(got_rhs, n_src, 1),
                      pair_sum(got_rhs, n_src, 0), halo, knots, me, count)
    right = [jnp.where(valid, right[at : at + 1], 0.0) for at in range(3)]
    update = sweeps(diag, rows, lower, inverse, right)
    final = jnp.concatenate(update + [jnp.zeros((5, LANES), F32)], 0)
    finals[src] = final

    def fin_copy(number, owner):
        return remote(finals.at[owner], finals.at[owner], fin_send.at[number],
                      fin_recv.at[number], lax.rem(src + number, n_src), seg)

    def fin_start(number, carry):
        fin_copy(number, src).start()
        return carry

    lax.fori_loop(1, n_src, fin_start, 0)

    out_att[...] = pltpu.roll(final, LANES - halo, 1)[:3, :knots]
    att_store = pltpu.make_async_copy(out_att, att_to, out_sem.at[1])
    att_store.start()

    def res_store(number, block):
        sl = block_slice(block, width)
        return pltpu.make_async_copy(out_res.at[:, sl], res_to.at[:, sl], res_sem.at[number])

    def last_step(number, carry):
        block = lax.rem(src - number + n_src, n_src)
        sl = block_slice(block, width)

        @pl.when(number > 0)
        def _():
            fin_copy(number, block).wait_recv()

        splines = [spline[block, at : at + 1] for at in range(4)]
        att = attitude_lookup(finals[block], halo - 1, hot_knot[block], splines, ad[:, sl])
        out_res[:, sl] = res[:, sl] - live_weight(corr[:, sl] + att, cnt[0, block])
        res_store(number, block).start()
        return carry

    lax.fori_loop(0, n_src, last_step, 0)

    def fin_sent(number, carry):
        fin_copy(number, src).wait_send()
        return carry

    lax.fori_loop(1, n_src, fin_sent, 0)
    for step in range(1, n_seg):
        sum_copy(step).wait_send()
        upd_copy(step, seg).wait_send()
    for slot in range(2):
        beside_copy(slot).wait_send()

    def norm_sent(number, carry):
        norm_copy(number, lax.rem(src + number, n_src)).wait_send()
        return carry

    lax.fori_loop(1, n_src, norm_sent, 0)
    knot_sent(*rhs_set)
    upd_store.wait()
    att_store.wait()

    def res_stored(number, carry):
        res_store(number, lax.rem(src - number + n_src, n_src)).wait()
        return carry

    lax.fori_loop(0, n_src, res_stored, 0)


def hand_over(a, b, c, a_to, b_to, c_to):
    a_to[...] = a[...]
    b_to[...] = b[...]
    c_to[...] = c[...]


def body(residual, obs_weight, time_frac, src_partials, att_dir, src_prior, att_prior,
         obs_source, obs_interval, obs_count):
    n_src = lax.axis_size("src")
    n_seg = lax.axis_size("seg")
    obs = residual.shape[0]
    sources = src_prior.shape[1]
    knots = att_prior.shape[1]
    groups = sources // LO
    share = groups // n_seg
    width = obs // n_src
    row = lambda x: x.reshape(1, obs)
    ints = pltpu.VMEM((1, obs), jnp.int32)
    line = pltpu.VMEM((1, obs), F32)
    dma = pltpu.SemaphoreType.DMA
    anywhere = pl.BlockSpec(memory_space=pl.ANY)
    outs = [jax.ShapeDtypeStruct(shape, F32) for shape in ((5, sources), (3, knots), (1, obs))]
    made = pl.pallas_call(
        functools.partial(update_kernel, n_src, n_seg, knots, 32),
        out_shape=outs,
        in_specs=[anywhere] * 9 + [smem],
        out_specs=[anywhere] * 3,
        scratch_shapes=[
            pltpu.VMEM((5, sources), F32), pltpu.VMEM((3, knots), F32), line,
            line, line, line, pltpu.VMEM((5, obs), F32), pltpu.VMEM((3, obs), F32), ints, ints,
            pltpu.VMEM((5, sources), F32), pltpu.VMEM((3, knots), F32),
            pltpu.VMEM((groups * 48, LO), F32),
            pltpu.VMEM((groups, 24, LO), F32),
            pltpu.VMEM((n_seg - 1, share, 24, LO), F32),
            pltpu.VMEM((groups, 8, LO), F32),
            pltpu.VMEM((n_src, 24, LANES), F32),
            pltpu.VMEM((n_src - 1, 24, LANES), F32),
            pltpu.VMEM((24, LANES), F32),
            pltpu.VMEM((2, 24, LANES), F32),
            pltpu.VMEM((n_src, 4, LANES), F32),
            pltpu.VMEM((3, n_src, 4, LANES), F32),
            pltpu.VMEM((n_src, 8, LANES), F32),
            pltpu.VMEM((n_src, LO, width), BF16),
            pltpu.VMEM((n_src, LANES, width), BF16),
            pltpu.VMEM((n_src, 4, width), F32),
            line,
            dma((9,)), dma((2,)), dma((n_src,)), dma((n_seg - 1,)), dma((n_seg - 1,)), dma((n_seg - 1,)), dma((n_seg - 1,)),
            dma((n_src - 1,)), dma((n_src - 1,)), dma((2,)), dma((2,)),
            dma((3, n_src)), dma((3, n_src)),
            dma((n_src,)), dma((n_src,)),
        ],
        compiler_params=pltpu.CompilerParams(
            collective_id=0, has_side_effects=True, vmem_limit_bytes=56 * 2**20
        ),
    )(row(residual), row(obs_weight), row(time_frac), src_partials, att_dir, row(obs_source),
      row(obs_interval), src_prior, att_prior, obs_count)
    src_update, att_update, out = pl.pallas_call(
        hand_over,
        out_shape=outs,
        in_specs=[vmem] * 3,
        out_specs=[vmem] * 3,
        compiler_params=pltpu.CompilerParams(vmem_limit_bytes=56 * 2**20),
    )(*made)
    return src_update, att_update, out.reshape(obs)


def solution(mesh):
    both = P(("src", "seg"))
    wide = P(None, ("src", "seg"))
    in_specs = (both, both, both, wide, wide, P(None, "src"), wide, both, both,
                P(("src", "seg"), None))
    out_specs = (P(None, "src"), wide, both)
    return jax.shard_map(body, mesh=mesh, in_specs=in_specs, out_specs=out_specs, check_vma=False)
```
